256 devices in a mesh: dp: 32 (over z_hi, y, core), cls: 8 (over x, z_lo).
Axes of the slice: x: 4, y: 4, z: 8 (z_hi: 4, z_lo: 2; z = z_hi * 2 + z_lo), core: 2. Of those that a mesh axis runs over, the one named last changes fastest.
Arguments:
- features: bfloat16 [16384, 1024], P('dp'), may hold values from -6 to 6
- labels: int32 [16384], P('dp'), may hold values from 0 to 11263
- inducing: bfloat16 [2048, 1024], P('cls'), may hold values from -6 to 6
- mean_weights: bfloat16 [2048, 11264], P('dp', 'cls'), may hold values from -0.125 to 0.125
- class_variance: float32 [11264], P('cls'), may hold values from 0.25 to 4
- class_rate: float32 [11264], P('cls'), may hold values from 0.2 to 10, as said below
Outputs:
- first_stats: float32 [2048, 11264], P('dp', 'cls')
- second_stats: float32 [2048, 11264], P('dp', 'cls')
The draws below stay inside these ranges and needn't reach their ends.
Inputs may be any that keep to these rules, and one draw needn't show every extreme that they name: `class_rate`: positive class weights.
All inputs are finite; a program needn't handle non-finite values.
Results may differ from the reference program's by a relative error of at most 0.0049.
Values may be sent and summed in bfloat16 or wider, within the bound.
No kernel may reach another device: no remote copies, remote signals or barrier semaphores. Data moves between devices by JAX's collectives and lax.ppermute only.
A program may use at most 128 MiB of HBM per device.

```python
import math
import jax
import jax.numpy as jnp
from jax import lax

D = 1024
INDUCING = 2048
ROWS = 512
TOKENS = 16384
CLASSES = 11264
N_DP = 32


def draw_class_rate(key, part):
    key = jax.random.fold_in(key, 7)
    place = jnp.arange(CLASSES, dtype=jnp.float32) / CLASSES
    rough = jax.random.uniform(key, (CLASSES,), jnp.float32, -0.7, 0.7)
    growth = 3.0
    return 0.5 * jnp.power(growth, place) * jnp.exp(rough)


def plant(result, stream_key, low, top_value):
    index_at = [jax.random.randint(jax.random.fold_in(stream_key, axis), (), 0, length) for axis, length in enumerate(result.shape)]
    widest = result.shape.index(max(result.shape))
    next_to = index_at[:widest] + [(index_at[widest] + 1) % result.shape[widest]] + index_at[widest + 1:]
    return result.at[tuple(index_at)].set(low).at[tuple(next_to)].set(top_value)


def level_of(own_key, extent, shards, smallest, top_value):
    gain, own = 1.0, jax.random.fold_in(own_key, 6)
    for axis_at, parts in shards:
        heights = jnp.exp(jax.random.uniform(jax.random.fold_in(own, axis_at), (parts,), jnp.float32, smallest / len(shards), top_value / len(shards)))
        gain = gain * jnp.repeat(heights, extent[axis_at] // parts).reshape([-1 if axis == axis_at else 1 for axis in range(len(extent))])
    return gain


def gaussian(rng, shape, scale, reach, pieces=(), kind=jnp.bfloat16):
    drawn = jax.random.normal(rng, shape, jnp.float32) * scale
    if len(pieces) > 0:
        drawn = level_of(rng, shape, pieces, -0.22, 0.18) * drawn
    return jnp.clip(drawn, min=-reach, max=reach).astype(kind)


def setup_inputs(seed: int = 0) -> dict:
    key_list = jax.random.split(jax.random.key(seed), 7)
    features = gaussian(key_list[0], (TOKENS, D), 1.0, 6.0, ((0, 32),))
    labels = plant(jax.random.randint(key_list[1], (TOKENS,), 0, CLASSES), jax.random.fold_in(key_list[1], 1), 0, CLASSES - 1).astype(jnp.int32)
    inducing = gaussian(key_list[2], (INDUCING, D), 1.0, 6.0, ((0, 8),))
    mean_weights = gaussian(key_list[3], (INDUCING, CLASSES), INDUCING ** -0.5, 0.125, ((0, 32), (1, 8)))
    class_variance = jnp.clip(jnp.exp(math.log(4.0) - 2.7725887 * jax.random.uniform(key_list[4], (CLASSES,), jnp.float32) ** level_of(key_list[4], (CLASSES,), ((0, 8),), -0.2, 0.2)), 0.25, 4.0)
    class_rate = draw_class_rate(jax.random.fold_in(key_list[6], 71), 0)
    return dict(features=features, labels=labels, inducing=inducing, mean_weights=mean_weights, class_variance=class_variance, class_rate=class_rate)


def normalized(rows):
    values = rows.astype(jnp.float32)
    scale = lax.rsqrt(lax.optimization_barrier(jnp.mean(values * values, axis=-1, keepdims=True)) + 1e-06)
    return (values * scale).astype(jnp.bfloat16)

def reference(features, labels, inducing, mean_weights, class_variance, class_rate):
    unit_points = normalized(inducing)
    factor = 1.0 / jnp.sqrt(jnp.float32(D))
    blocks = features.reshape(N_DP, ROWS, D)
    label_blocks = labels.reshape(N_DP, ROWS)
    class_ids = jnp.arange(CLASSES, dtype=jnp.int32)

    def one_block(carry, item):
        feats, labs = item
        unit_rows = normalized(feats)
        dots = lax.dot_general(unit_rows, unit_points, (((1,), (1,)), ((), ())), preferred_element_type=jnp.float32)
        kernel = jnp.exp(dots * factor).astype(jnp.bfloat16)
        kernel_wide = kernel.astype(jnp.float32)
        kernel_sq = (kernel_wide * kernel_wide).astype(jnp.bfloat16)
        means = jnp.dot(kernel, mean_weights, preferred_element_type=jnp.float32)
        spread = jnp.sqrt(means * means + class_variance[None, :])
        ratio = class_rate[None, :] * jnp.exp(-(means + spread) * 0.5) / (1.0 + jnp.exp(-spread))
        total = lax.optimization_barrier(jnp.sum(ratio, axis=1))
        intensity = (1.0 + total) / (1.0 + 0.5 * CLASSES)
        expected = intensity[:, None] * ratio
        onehot = (labs[:, None] == class_ids[None, :]).astype(jnp.float32)
        first_weight = ((onehot - expected) * 0.5).astype(jnp.bfloat16)
        second_weight = ((onehot + expected) * jnp.tanh(spread * 0.5) / (2.0 * spread)).astype(jnp.bfloat16)
        part_one = lax.dot_general(kernel, first_weight, (((0,), (0,)), ((), ())), preferred_element_type=jnp.float32)
        part_two = lax.dot_general(kernel_sq, second_weight, (((0,), (0,)), ((), ())), preferred_element_type=jnp.float32)
        return ((carry[0] + part_one, carry[1] + part_two), None)
    start = (jnp.zeros((INDUCING, CLASSES), jnp.float32), jnp.zeros((INDUCING, CLASSES), jnp.float32))
    sums, unused = lax.scan(one_block, start, (blocks, label_blocks))
    return (sums[0] / TOKENS, sums[1] / TOKENS)
```

```python
import jax
import jax.numpy as jnp
from jax import lax
from jax.sharding import Mesh, PartitionSpec as P

SIZE = {"zh": 4, "y": 4, "c": 2, "x": 4, "zl": 2}
AXES = tuple(SIZE)
BF = jnp.bfloat16
F32 = jnp.float32


def swap(value, **masks):
    names = tuple(a for a in AXES if a in masks)
    pairs, count = [], 1
    for a in names:
        count *= SIZE[a]
    for i in range(count):
        left, at = i, {}
        for a in reversed(names):
            at[a] = left % SIZE[a]
            left //= SIZE[a]
        j = 0
        for a in names:
            j = j * SIZE[a] + (at[a] ^ masks[a])
        pairs.append((i, j))
    return lax.ppermute(value, names, pairs)


def ring_gather(value, axis):
    near = swap(value, **{axis: 1})
    back = swap(value, **{axis: 3})
    half = value.shape[0] // 2
    far_a = swap(near[:half], **{axis: 3})
    far_b = swap(back[half:], **{axis: 1})
    return [value, near, (far_a, far_b), back]


def normalized(rows):
    values = rows.astype(F32)
    scale = lax.rsqrt(jnp.mean(values * values, axis=-1, keepdims=True) + 1e-06)
    return (values * scale).astype(BF)


def body(features, labels, inducing, mean_weights, class_variance, class_rate):
    zh, y, c, x, zl = (lax.axis_index(a) for a in AXES)
    width = features.shape[1]
    factor = 1.0 / jnp.sqrt(F32(width))
    all_local = mean_weights.shape[1]
    half = all_local // 2
    slab = 128

    points = normalized(inducing)
    mine = lax.dynamic_slice_in_dim(points, c * slab, slab, 0)
    pair = jnp.concatenate([mine, swap(mine, zl=1)], axis=0)

    keep = lax.dynamic_slice_in_dim(mean_weights, c * half, half, 1)
    give = lax.dynamic_slice_in_dim(mean_weights, (1 - c) * half, half, 1)
    got = swap(give, c=1)
    block = jnp.where(c == 0, jnp.concatenate([keep, got], 0), jnp.concatenate([got, keep], 0))

    unit_rows = normalized(features)
    rows = jnp.concatenate([unit_rows, swap(unit_rows, c=1)], axis=0)
    labs = jnp.concatenate([labels, swap(labels, c=1)], axis=0)

    near, back = swap(pair, x=1), swap(pair, x=3)
    own_y = ring_gather(block, "y")
    others_z = jnp.concatenate([swap(block, zh=1), swap(block, zh=2), swap(block, zh=3)], 0)
    rest_y = ring_gather(others_z, "y")
    far = jnp.concatenate([swap(near[:slab], x=3), swap(back[slab:], x=1)], 0)

    table = jnp.zeros((16, slab, width), BF)
    for kx, piece in ((0, pair), (1, near), (3, back), (2, far)):
        for core, part in ((c, piece), (1 - c, swap(piece, c=1))):
            for kl in range(2):
                kz = zh ^ x ^ kx
                ky = y ^ ((zl ^ kl) * 2 + core)
                table = lax.dynamic_update_slice(
                    table, part[None, kl * slab : (kl + 1) * slab], (ky * 4 + kz, 0, 0)
                )
    table = table.reshape(16 * slab, width)
    dots = lax.dot_general(rows, table, (((1,), (1,)), ((), ())), preferred_element_type=F32)
    kernel = jnp.exp(dots * factor).astype(BF)
    wide = kernel.astype(F32)
    kernel_sq = (wide * wide).astype(BF)

    weights = []
    for ky in range(4):
        own, rest = own_y[ky], rest_y[ky]
        if ky == 2:
            own, rest = jnp.concatenate(own, 0), jnp.concatenate(rest, 0)
        weights += [own, rest]
    weights = jnp.concatenate(weights, 0)

    variance = lax.dynamic_slice_in_dim(class_variance, c * half, half, 0)
    rate = lax.dynamic_slice_in_dim(class_rate, c * half, half, 0)
    means = jnp.dot(kernel, weights, preferred_element_type=F32)
    spread = jnp.sqrt(means * means + variance[None, :])
    ratio = rate[None, :] * jnp.exp(-(means + spread) * 0.5) / (1.0 + jnp.exp(-spread))
    total = jnp.sum(ratio, axis=1).reshape(2, 4, 128)
    turn = total[::-1]
    total = total + swap(total, zl=1) + (swap(turn, c=1) + swap(turn, c=1, zl=1))
    total = (total + swap(total, x=2)) + (swap(total, x=1) + swap(total, x=3))
    total = total.reshape(-1)
    all_classes = all_local * 8
    intensity = (1.0 + total) / (1.0 + 0.5 * all_classes)
    expected = intensity[:, None] * ratio
    offset = (x * 2 + zl) * all_local + c * half
    class_ids = offset + jnp.arange(half, dtype=jnp.int32)
    onehot = (labs[:, None] == class_ids[None, :]).astype(F32)
    first_weight = ((onehot - expected) * 0.5).astype(BF)
    second_weight = ((onehot + expected) * jnp.tanh(spread * 0.5) / (2.0 * spread)).astype(BF)

    def stats(which, ky, kzs):
        left, right = ((kernel, first_weight), (kernel_sq, second_weight))[which]
        at = [(ky * 4 + kz) * slab for kz in kzs]
        cols = jnp.concatenate([left[:, a : a + slab] for a in at], 1) if len(at) > 1 else left[:, at[0] : at[0] + slab]
        return lax.dot_general(cols, right, (((0,), (0,)), ((), ())), preferred_element_type=F32)

    def reduce_y(kzs):
        far_one = swap(stats(0, 2, kzs).astype(BF), y=1)
        far_two = swap(stats(1, 2, kzs).astype(BF), y=3)
        one_near = swap(stats(0, 1, kzs).astype(BF), y=1)
        two_back = swap(stats(1, 3, kzs).astype(BF), y=3)
        one_back = swap((stats(0, 3, kzs) + far_one.astype(F32)).astype(BF), y=3)
        two_near = swap((stats(1, 1, kzs) + far_two.astype(F32)).astype(BF), y=1)
        one = stats(0, 0, kzs) + one_near.astype(F32) + one_back.astype(F32)
        two = stats(1, 0, kzs) + two_near.astype(F32) + two_back.astype(F32)
        return one, two

    one2, two2 = reduce_y((2,))
    z2 = swap(jnp.stack([one2, two2]).astype(BF), zh=2)
    one13, two13 = reduce_y((1, 3))
    z1 = swap(jnp.stack([one13[:slab], two13[:slab]]).astype(BF), zh=1)
    z3 = swap(jnp.stack([one13[slab:], two13[slab:]]).astype(BF), zh=3)
    one0, two0 = reduce_y((0,))
    summed = jnp.stack([one0, two0]) + (z2.astype(F32) + z1.astype(F32) + z3.astype(F32))
    summed = summed * (1.0 / (1024 * 16))
    mine = lax.dynamic_slice_in_dim(summed, c * 64, 64, 1)
    theirs = swap(lax.dynamic_slice_in_dim(summed, (1 - c) * 64, 64, 1), c=1)
    out = jnp.where(c == 0, jnp.concatenate([mine, theirs], 2), jnp.concatenate([theirs, mine], 2))
    return out[0], out[1]


def solution(mesh):
    parts = Mesh(mesh.devices.reshape(tuple(SIZE.values())), AXES)
    dp, cls = ("zh", "y", "c"), ("x", "zl")
    in_specs = (P(dp, None), P(dp), P(cls, None), P(dp, cls), P(cls), P(cls))
    out_specs = (P(dp, cls), P(dp, cls))
    return jax.shard_map(body, mesh=parts, in_specs=in_specs, out_specs=out_specs, check_vma=False)
```

```python
import jax
import jax.numpy as jnp
from jax import lax
from jax.experimental import pallas as pl
from jax.experimental.pallas import tpu as pltpu
from jax.sharding import Mesh, PartitionSpec as P

SIZE = {"zh": 4, "y": 4, "c": 2, "x": 4, "zl": 2}
AXES = tuple(SIZE)
BF = jnp.bfloat16
F32 = jnp.float32
SLAB = 128
PART = 64


def swap(value, **masks):
    names = tuple(a for a in AXES if a in masks)
    pairs, count = [], 1
    for a in names:
        count *= SIZE[a]
    for i in range(count):
        left, at = i, {}
        for a in reversed(names):
            at[a] = left % SIZE[a]
            left //= SIZE[a]
        j = 0
        for a in names:
            j = j * SIZE[a] + (at[a] ^ masks[a])
        pairs.append((i, j))
    return lax.ppermute(value, names, pairs)


def normalized(rows):
    values = rows.astype(F32)
    scale = lax.rsqrt(jnp.mean(values * values, axis=-1, keepdims=True) + 1e-06)
    return (values * scale).astype(BF)


def kernel_rows(places, rows, relayed, points):
    width = rows.shape[1]
    own = rows.shape[0]
    step = 256
    factor = 1.0 / float(width) ** 0.5

    def body(*refs):
        place, row_ref = refs[0], refs[1]
        relay_refs, point_refs = refs[2:6], refs[6:14]
        out, out_sq, held = refs[14:]
        held[:own] = row_ref[...]
        for kx in range(4):
            for kl in range(2):
                at = pl.multiple_of(place[16 + kx * 2 + kl] * PART, PART)
                held[pl.ds(own + at, PART)] = relay_refs[kx][kl * PART : (kl + 1) * PART]

        @pl.loop(0, 2 * own // step)
        def _(i):
            block = pl.ds(pl.multiple_of(i * step, step), step)
            left = held[block]
            for n in range(8):
                dots = lax.dot_general(
                    left, point_refs[n][...], (((1,), (1,)), ((), ())), preferred_element_type=F32
                )
                value = jnp.exp(dots * factor).astype(BF)
                wide = value.astype(F32)
                square = (wide * wide).astype(BF)
                for kl in range(2):
                    to = pl.ds(pl.multiple_of(place[n * 2 + kl] * SLAB, SLAB), SLAB)
                    out[block, to] = value[:, kl * SLAB : (kl + 1) * SLAB]
                    out_sq[block, to] = square[:, kl * SLAB : (kl + 1) * SLAB]

    vmem = pl.BlockSpec(memory_space=pltpu.VMEM)
    shape = jax.ShapeDtypeStruct((2 * own, 16 * SLAB), BF)
    return pl.pallas_call(
        body,
        out_shape=(shape, shape),
        in_specs=[pl.BlockSpec(memory_space=pltpu.SMEM)] + [vmem] * 13,
        out_specs=(vmem, vmem),
        scratch_shapes=[pltpu.VMEM((2 * own, width), BF)],
        compiler_params=pltpu.CompilerParams(vmem_limit_bytes=40 << 20),
        cost_estimate=pl.CostEstimate(
            flops=2 * 2 * own * 16 * SLAB * width, bytes_accessed=16 << 20, transcendentals=2 * own * 16 * SLAB
        ),
        name="kernel_rows",
    )(places, rows, *relayed, *points)


def body(features, labels, inducing, mean_weights, class_variance, class_rate):
    zh, y, c, x, zl = (lax.axis_index(a) for a in AXES)
    h = zh % 2
    all_local = mean_weights.shape[1]
    half = all_local // 2
    quarter = half // 2

    unit_rows = normalized(features)
    relay = swap(lax.dynamic_slice_in_dim(unit_rows, (x * 2 + zl) * PART, PART, 0), zh=1)
    points = normalized(inducing)
    mine = lax.dynamic_slice_in_dim(points, c * SLAB, SLAB, 0)
    pack = jnp.concatenate([mine, relay], 0)
    pair = jnp.concatenate([pack, swap(pack, zl=1)], 0)
    packs = [pair, swap(pair, x=1), swap(pair, x=2), swap(pair, x=3)]
    size = SLAB + PART

    local = mean_weights.T.reshape(2, 2, quarter, -1)
    keep = lax.dynamic_index_in_dim(local, c, 1, False)
    give = lax.dynamic_index_in_dim(local, 1 - c, 1, False)
    got = swap(give, c=1)
    block = jnp.where(c == 0, jnp.concatenate([keep, got], 2), jnp.concatenate([got, keep], 2))
    same = lax.dynamic_index_in_dim(block, h, 0, False)
    other = lax.dynamic_index_in_dim(block, 1 - h, 0, False)
    over_z = jnp.concatenate([same, swap(other, zh=1), swap(same, zh=2), swap(other, zh=3)], 1)
    over_y = jnp.concatenate([over_z, swap(over_z, y=1), swap(over_z, y=2), swap(over_z, y=3)], 1)
    theirs = swap(over_y, c=1)
    weights = jnp.where(c == 0, jnp.concatenate([over_y, theirs], 0), jnp.concatenate([theirs, over_y], 0))

    labs = jnp.concatenate([labels, swap(labels, zh=1)], 0)

    places, tables, relayed = [], [], []
    for kx, piece in enumerate(packs):
        held = jnp.concatenate([piece[:SLAB], piece[size : size + SLAB]], 0)
        relayed.append(jnp.concatenate([piece[SLAB:size], piece[size + SLAB :]], 0))
        for core, part in ((c, held), (1 - c, swap(held, c=1))):
            tables.append(part)
            for kl in range(2):
                places.append((y ^ ((zl ^ kl) * 2 + core)) * 4 + (zh ^ x ^ kx))
    for kx in range(4):
        for kl in range(2):
            places.append((x ^ kx) * 2 + (zl ^ kl))
    places = jnp.stack(places).astype(jnp.int32)
    kernel, kernel_sq = kernel_rows(places, unit_rows, relayed, tables)

    variance = lax.dynamic_slice_in_dim(class_variance, h * half, half, 0)[:, None]
    rate = lax.dynamic_slice_in_dim(class_rate, h * half, half, 0)[:, None]
    means = lax.dot_general(weights, kernel, (((1,), (1,)), ((), ())), preferred_element_type=F32)
    spread = jnp.sqrt(means * means + variance)
    ratio = rate * jnp.exp(-(means + spread) * 0.5) / (1.0 + jnp.exp(-spread))
    total = jnp.sum(ratio, axis=0).reshape(2, 4, 128)
    turn = total[::-1]
    total = total + swap(total, zl=1) + (swap(turn, zh=1) + swap(turn, zh=1, zl=1))
    total = (total + swap(total, x=2)) + (swap(total, x=1) + swap(total, x=3))
    total = total.reshape(1, -1)
    all_classes = all_local * 8
    intensity = (1.0 + total) / (1.0 + 0.5 * all_classes)
    expected = intensity * ratio
    offset = (x * 2 + zl) * all_local + h * half
    class_ids = offset + jnp.arange(half, dtype=jnp.int32)
    onehot = (class_ids[:, None] == labs[None, :]).astype(F32)
    first_weight = ((onehot - expected) * 0.5).astype(BF)
    second_weight = ((onehot + expected) * jnp.tanh(spread * 0.5) / (2.0 * spread)).astype(BF)

    def quarter_of(which, value):
        return lax.dynamic_slice_in_dim(value, which * quarter, quarter, 0)

    sums = []
    for left, right in ((first_weight, kernel), (second_weight, kernel_sq)):
        theirs = swap(jnp.dot(quarter_of(1 - c, left), right, preferred_element_type=F32).astype(BF), c=1)
        sums.append((jnp.dot(quarter_of(c, left), right, preferred_element_type=F32), theirs))

    halves = []
    for ours, theirs in sums:
        def chunk(ky):
            at = slice(ky * 512, (ky + 1) * 512)
            return ours[:, at] + theirs[:, at].astype(F32)

        near, back, far = (swap(chunk(ky).astype(BF), y=ky) for ky in (1, 3, 2))
        own = (chunk(0) + far.astype(F32)) + (near.astype(F32) + back.astype(F32))

        got = []
        for kz in (2, 1, 3):
            part = own[:, kz * SLAB : (kz + 1) * SLAB]
            middle = jnp.mean(part, axis=0, keepdims=True).astype(BF)
            rest = (part - middle.astype(F32)).astype(BF)
            sent = jnp.concatenate([rest, jnp.broadcast_to(middle, (16, SLAB))], 0)
            came = swap(sent, zh=kz).astype(F32)
            got.append(came[:quarter] + came[quarter : quarter + 1])
        halves.append(jnp.stack([own[:, :SLAB] + got[0], got[1] + got[2]]))

    summed = jnp.stack(halves) * (1.0 / (512 * 32))
    summed = summed.transpose(0, 3, 1, 2)
    mine = lax.dynamic_slice_in_dim(summed, c * 64, 64, 1)
    theirs = swap(lax.dynamic_slice_in_dim(summed, (1 - c) * 64, 64, 1), c=1)
    both = jnp.where(c == 0, jnp.stack([mine, theirs], 3), jnp.stack([theirs, mine], 3))
    both = jnp.where(h == 0, both, both[:, :, ::-1])
    out = both.reshape(2, 64, all_local)
    return out[0], out[1]


def solution(mesh):
    parts = Mesh(mesh.devices.reshape(tuple(SIZE.values())), AXES)
    dp, cls = ("zh", "y", "c"), ("x", "zl")
    in_specs = (P(dp, None), P(dp), P(cls, None), P(dp, cls), P(cls), P(cls))
    out_specs = (P(dp, cls), P(dp, cls))
    return jax.shard_map(body, mesh=parts, in_specs=in_specs, out_specs=out_specs, check_vma=False)
```

```python
import jax
import jax.numpy as jnp
from jax import lax
from jax.experimental import pallas as pl
from jax.experimental.pallas import tpu as pltpu
from jax.sharding import Mesh, PartitionSpec as P

SIZE = {"zh": 4, "y": 4, "c": 2, "x": 4, "zl": 2}
AXES = tuple(SIZE)
BF = jnp.bfloat16
F32 = jnp.float32
SLAB = 128
ORDER = (0, 1, 3, 2)
PART = 128


def swap(value, **masks):
    names = tuple(a for a in AXES if a in masks)
    pairs, count = [], 1
    for a in names:
        count *= SIZE[a]
    for i in range(count):
        left, at = i, {}
        for a in reversed(names):
            at[a] = left % SIZE[a]
            left //= SIZE[a]
        j = 0
        for a in names:
            j = j * SIZE[a] + (at[a] ^ masks[a])
        pairs.append((i, j))
    return lax.ppermute(value, names, pairs)


def normalized(rows):
    values = rows.astype(F32)
    scale = lax.rsqrt(jnp.mean(values * values, axis=-1, keepdims=True) + 1e-06)
    return (values * scale).astype(BF)


def kernel_rows(places, rows, relayed, tables):
    width = rows.shape[1]
    own = rows.shape[0]
    count = 2 * own if relayed else own
    many = len(tables)
    step = 256
    factor = 1.0 / float(width) ** 0.5

    def body(*refs):
        place, row_ref, refs = refs[0], refs[1], refs[2:]
        relay_refs, table_refs, refs = refs[: len(relayed)], refs[len(relayed) :][:many], refs[len(relayed) + many :]
        out, out_sq = refs[:2]
        held = row_ref
        if relayed:
            held = refs[2]
            held[:own] = row_ref[...]
            for kx in range(4):
                at = pl.multiple_of(place[2 * many + kx] * PART, PART)
                held[pl.ds(own + at, PART)] = relay_refs[kx][...]

        @pl.loop(0, count // step)
        def _(i):
            block = pl.ds(pl.multiple_of(i * step, step), step)
            left = held[block]
            for n in range(many):
                dots = lax.dot_general(
                    left, table_refs[n][...], (((1,), (1,)), ((), ())), preferred_element_type=F32
                )
                value = jnp.exp(dots * factor).astype(BF)
                wide = value.astype(F32)
                square = (wide * wide).astype(BF)
                for kl in range(2):
                    to = pl.ds(pl.multiple_of(place[n * 2 + kl] * SLAB, SLAB), SLAB)
                    out[block, to] = value[:, kl * SLAB : (kl + 1) * SLAB]
                    out_sq[block, to] = square[:, kl * SLAB : (kl + 1) * SLAB]

    vmem = pl.BlockSpec(memory_space=pltpu.VMEM)
    shape = jax.ShapeDtypeStruct((count, 2 * many * SLAB), BF)
    given = [places, rows, *relayed, *tables]
    return pl.pallas_call(
        body,
        out_shape=(shape, shape) + ((jax.ShapeDtypeStruct((count, width), BF),) if relayed else ()),
        in_specs=[pl.BlockSpec(memory_space=pltpu.SMEM)] + [vmem] * (len(given) - 1),
        out_specs=(vmem, vmem) + ((vmem,) if relayed else ()),
        compiler_params=pltpu.CompilerParams(vmem_limit_bytes=40 << 20),
        cost_estimate=pl.CostEstimate(
            flops=2 * count * 2 * many * SLAB * width,
            bytes_accessed=count * 2 * many * SLAB * 4,
            transcendentals=count * 2 * many * SLAB,
        ),
        name="kernel_rows",
    )(*given)


def body(features, labels, inducing, mean_weights, class_variance, class_rate):
    zh, y, c, x, zl = (lax.axis_index(a) for a in AXES)
    h = zh % 2
    all_local = mean_weights.shape[1]
    half = all_local // 2
    quarter = half // 2

    mine = normalized(lax.dynamic_slice_in_dim(inducing, c * SLAB, SLAB, 0))
    pair = jnp.concatenate([mine, swap(mine, zl=1)], 0)

    relay = swap(normalized(lax.dynamic_slice_in_dim(features, x * PART, PART, 0)), zh=1)

    local = mean_weights.T.reshape(2, 2, quarter, -1)
    keep = lax.dynamic_index_in_dim(local, c, 1, False)
    give = lax.dynamic_index_in_dim(local, 1 - c, 1, False)
    got = swap(give, c=1)
    block = jnp.where(c == 0, jnp.concatenate([keep, got], 2), jnp.concatenate([got, keep], 2))
    spread_out = lax.dynamic_index_in_dim(lax.all_gather(block, ("y", "zh")), h, 1, False)
    spread_out = spread_out.reshape(4, 4, quarter, SLAB)
    by_kx = [lax.dynamic_index_in_dim(spread_out, x ^ kx, 1, False) for kx in ORDER]
    ours = jnp.concatenate([by_kx[i][k] for k in range(4) for i in range(3)] + list(by_kx[3]), 1)
    theirs = swap(ours, c=1)
    weights = jnp.where(c == 0, jnp.concatenate([ours, theirs], 0), jnp.concatenate([theirs, ours], 0))

    labs = jnp.concatenate([labels, swap(labels, zh=1)], 0)

    pack = jnp.concatenate([pair, relay], 0)
    near, back = swap(pack, x=1), swap(pack, x=3)
    relay_far, near, back = lax.optimization_barrier((swap(relay, x=2), near, back))
    relayed = [relay, near[2 * SLAB :], relay_far, back[2 * SLAB :]]
    near, back = near[: 2 * SLAB], back[: 2 * SLAB]
    far = [swap(near[:SLAB], x=3), swap(back[SLAB:], x=1)]

    def places(order):
        found = []
        for i, kx in enumerate(order):
            for core in (c, 1 - c):
                for kl in range(2):
                    found.append(((zl ^ kl) * 2 + core) * len(order) + i)
        return found

    where = jnp.stack(places(ORDER[:3]) + [x ^ kx for kx in range(4)]).astype(jnp.int32)
    tables = [pair, swap(pair, c=1), near, swap(near, c=1), back, swap(back, c=1)]
    near_k, near_sq, rows = kernel_rows(where, normalized(features), relayed, tables)
    cut = 12 * SLAB
    near_means = lax.dot_general(weights[:, :cut], near_k, (((1,), (1,)), ((), ())), preferred_element_type=F32)
    far, rows, near_means = lax.optimization_barrier((far, rows, near_means))
    where = jnp.stack(places(ORDER[3:])).astype(jnp.int32)
    last = jnp.concatenate(far, 0)
    last_k, last_sq = kernel_rows(where, rows, [], [last, swap(last, c=1)])
    last_means = lax.dot_general(weights[:, cut:], last_k, (((1,), (1,)), ((), ())), preferred_element_type=F32)

    variance = lax.dynamic_slice_in_dim(class_variance, h * half, half, 0)[:, None]
    rate = lax.dynamic_slice_in_dim(class_rate, h * half, half, 0)[:, None]
    means = near_means + last_means
    spread = jnp.sqrt(means * means + variance)
    ratio = rate * jnp.exp(-(means + spread) * 0.5) / (1.0 + jnp.exp(-spread))
    total = jnp.sum(ratio, axis=0).reshape(2, 4, 128)
    turn = total[::-1]
    total = total + swap(total, zl=1) + (swap(turn, zh=1) + swap(turn, zh=1, zl=1))
    total = (total + swap(total, x=2)) + (swap(total, x=1) + swap(total, x=3))
    total = total.reshape(1, -1)
    all_classes = all_local * 8
    intensity = (1.0 + total) / (1.0 + 0.5 * all_classes)
    expected = intensity * ratio
    offset = (x * 2 + zl) * all_local + h * half
    class_ids = offset + jnp.arange(half, dtype=jnp.int32)
    onehot = (class_ids[:, None] == labs[None, :]).astype(F32)
    first_weight = ((onehot - expected) * 0.5).astype(BF)
    second_weight = ((onehot + expected) * jnp.tanh(spread * 0.5) / (2.0 * spread)).astype(BF)

    def quarter_of(which, value):
        return lax.dynamic_slice_in_dim(value, which * quarter, quarter, 0)

    sums = []
    for left, pieces in ((first_weight, (near_k, last_k)), (second_weight, (near_sq, last_sq))):
        give, keep = quarter_of(1 - c, left), quarter_of(c, left)
        theirs = [swap(jnp.dot(give, p, preferred_element_type=F32).astype(BF), c=1) for p in pieces]
        sums.append(([jnp.dot(keep, p, preferred_element_type=F32) for p in pieces], theirs))

    halves, before = [], ()
    for which, (ours, theirs) in enumerate(sums):
        def chunk(ky):
            parts = []
            for kept, came in zip(ours, theirs):
                size = kept.shape[1] // 4
                at = (y ^ ky) * size
                parts.append(
                    lax.dynamic_slice_in_dim(kept, at, size, 1)
                    + lax.dynamic_slice_in_dim(came, at, size, 1).astype(F32)
                )
            return jnp.concatenate(parts, 1)

        came = tuple(swap(chunk(ky).astype(BF), y=ky) for ky in (1, 3, 2))
        came, before = lax.optimization_barrier((came, before))
        near, back, far = (value.astype(F32) for value in came)
        own = ((chunk(0) + far) + (near + back)).T
        middle = jnp.mean(own, axis=0, keepdims=True).astype(BF)
        rest = (own - middle.astype(F32)).astype(BF)
        tail = jnp.broadcast_to(middle, (16, quarter))

        def slab_of(value, kz):
            kx = x ^ zh ^ kz
            return lax.dynamic_slice_in_dim(value, (kx ^ (kx // 2)) * SLAB, SLAB, 0)

        def widen(value):
            return value[:-16].astype(F32) + value[-1:].astype(F32)

        if which == 0:
            got = swap(jnp.concatenate([slab_of(rest, 2), slab_of(rest, 3), tail], 0), zh=2)
            before = (got,)
            got = widen(got)
            mine = slab_of(own, 0) + got[:SLAB]
            give = slab_of(own, 1) + got[SLAB:]
            middle = jnp.mean(give, axis=0, keepdims=True).astype(BF)
            rest = (give - middle.astype(F32)).astype(BF)
            give = jnp.concatenate([rest, jnp.broadcast_to(middle, (16, quarter))], 0)
            halves.append(jnp.stack([mine, widen(swap(give, zh=1))], 1))
        else:
            send = [jnp.concatenate([slab_of(rest, kz), tail], 0) for kz in (2, 1, 3)]
            send = lax.optimization_barrier(send)
            got = [swap(value, zh=kz) for value, kz in zip(send, (2, 1, 3))]
            got = [widen(value) for value in lax.optimization_barrier(got)]
            halves.append(jnp.stack([slab_of(own, 0) + got[0], got[1] + got[2]], 1))

    summed = jnp.stack(halves) * (1.0 / (512 * 32))
    mine = lax.dynamic_slice_in_dim(summed, c * 64, 64, 1)
    theirs = swap(lax.dynamic_slice_in_dim(summed, (1 - c) * 64, 64, 1), c=1)
    both = jnp.where(c == 0, jnp.stack([mine, theirs], 3), jnp.stack([theirs, mine], 3))
    both = jnp.where(h == 0, both, both[:, :, ::-1])
    out = both.reshape(2, 64, all_local)
    return out[0], out[1]


def solution(mesh):
    parts = Mesh(mesh.devices.reshape(tuple(SIZE.values())), AXES)
    dp, cls = ("zh", "y", "c"), ("x", "zl")
    in_specs = (P(dp, None), P(dp), P(cls, None), P(dp, cls), P(cls), P(cls))
    out_specs = (P(dp, cls), P(dp, cls))
    return jax.shard_map(body, mesh=parts, in_specs=in_specs, out_specs=out_specs, check_vma=False)
```

```python
import jax
import jax.numpy as jnp
from jax import lax
from jax.experimental import pallas as pl
from jax.experimental.pallas import tpu as pltpu
from jax.sharding import Mesh, PartitionSpec as P

SIZE = {"zh": 4, "y": 4, "c": 2, "x": 4, "zl": 2}
AXES = tuple(SIZE)
BF = jnp.bfloat16
F32 = jnp.float32
SLAB = 128
ORDER = (0, 1, 3, 2)
PART = 128


def swap(value, **masks):
    names = tuple(a for a in AXES if a in masks)
    pairs, count = [], 1
    for a in names:
        count *= SIZE[a]
    for i in range(count):
        left, at = i, {}
        for a in reversed(names):
            at[a] = left % SIZE[a]
            left //= SIZE[a]
        j = 0
        for a in names:
            j = j * SIZE[a] + (at[a] ^ masks[a])
        pairs.append((i, j))
    return lax.ppermute(value, names, pairs)


def normalized(rows):
    values = rows.astype(F32)
    scale = lax.rsqrt(jnp.mean(values * values, axis=-1, keepdims=True) + 1e-06)
    return (values * scale).astype(BF)


def kernel_rows(places, rows, relayed, tables):
    width = rows.shape[1]
    own = rows.shape[0]
    count = 2 * own if relayed else own
    many = len(tables)
    step = 256
    factor = 1.0 / float(width) ** 0.5

    def body(*refs):
        place, row_ref, refs = refs[0], refs[1], refs[2:]
        relay_refs, table_refs, refs = refs[: len(relayed)], refs[len(relayed) :][:many], refs[len(relayed) + many :]
        out, out_sq = refs[:2]
        held = row_ref
        if relayed:
            held = refs[2]
            held[:own] = row_ref[...]
            for kx in range(4):
                at = pl.multiple_of(place[2 * many + kx] * PART, PART)
                held[pl.ds(own + at, PART)] = relay_refs[kx][...]

        @pl.loop(0, count // step)
        def _(i):
            block = pl.ds(pl.multiple_of(i * step, step), step)
            left = held[block]
            for n in range(many):
                dots = lax.dot_general(
                    left, table_refs[n][...], (((1,), (1,)), ((), ())), preferred_element_type=F32
                )
                value = jnp.exp(dots * factor).astype(BF)
                wide = value.astype(F32)
                square = (wide * wide).astype(BF)
                for kl in range(2):
                    to = pl.ds(pl.multiple_of(place[n * 2 + kl] * SLAB, SLAB), SLAB)
                    out[block, to] = value[:, kl * SLAB : (kl + 1) * SLAB]
                    out_sq[block, to] = square[:, kl * SLAB : (kl + 1) * SLAB]

    vmem = pl.BlockSpec(memory_space=pltpu.VMEM)
    shape = jax.ShapeDtypeStruct((count, 2 * many * SLAB), BF)
    given = [places, rows, *relayed, *tables]
    return pl.pallas_call(
        body,
        out_shape=(shape, shape) + ((jax.ShapeDtypeStruct((count, width), BF),) if relayed else ()),
        in_specs=[pl.BlockSpec(memory_space=pltpu.SMEM)] + [vmem] * (len(given) - 1),
        out_specs=(vmem, vmem) + ((vmem,) if relayed else ()),
        compiler_params=pltpu.CompilerParams(vmem_limit_bytes=40 << 20),
        cost_estimate=pl.CostEstimate(
            flops=2 * count * 2 * many * SLAB * width,
            bytes_accessed=count * 2 * many * SLAB * 4,
            transcendentals=count * 2 * many * SLAB,
        ),
        name="kernel_rows",
    )(*given)


def body(features, labels, inducing, mean_weights, class_variance, class_rate):
    zh, y, c, x, zl = (lax.axis_index(a) for a in AXES)
    h = zh % 2
    all_local = mean_weights.shape[1]
    half = all_local // 2
    quarter = half // 2

    mine = normalized(lax.dynamic_slice_in_dim(inducing, c * SLAB, SLAB, 0))
    relay = normalized(lax.dynamic_slice_in_dim(features, x * PART, PART, 0))
    mine, relay, mean_weights = lax.optimization_barrier((mine, relay, mean_weights))
    relay = swap(relay, zh=1)
    pair = jnp.concatenate([mine, swap(mine, zl=1)], 0)

    local = mean_weights.T.reshape(2, 2, quarter, -1)
    keep = lax.dynamic_index_in_dim(local, c, 1, False)
    give = lax.dynamic_index_in_dim(local, 1 - c, 1, False)
    got = swap(give, c=1)
    block = jnp.where(c == 0, jnp.concatenate([keep, got], 2), jnp.concatenate([got, keep], 2))
    same = lax.dynamic_index_in_dim(block, h, 0, False)
    other = lax.dynamic_index_in_dim(block, 1 - h, 0, False)
    over_z = jnp.stack([same, swap(other, zh=1), swap(same, zh=2), swap(other, zh=3)])

    pack = jnp.concatenate([pair, relay], 0)
    near, back = swap(pack, x=1), swap(pack, x=3)
    relay_far, near, back = lax.optimization_barrier((swap(relay, x=2), near, back))
    relayed = [relay, near[2 * SLAB :], relay_far, back[2 * SLAB :]]
    near, back = near[: 2 * SLAB], back[: 2 * SLAB]
    far = [swap(near[:SLAB], x=3), swap(back[SLAB:], x=1)]

    over_z = jnp.concatenate([lax.dynamic_index_in_dim(over_z, zh ^ x ^ kx, 0, False) for kx in ORDER], 1)
    over_z, pack = lax.optimization_barrier((over_z, pack))
    over_y = [over_z, swap(over_z, y=1), None, swap(over_z, y=3)]
    over_z, over_y[1], over_y[3], relay_far = lax.optimization_barrier((over_z, over_y[1], over_y[3], relay_far))
    over_y[2] = swap(over_z, y=2)
    cut = 3 * SLAB
    ours = jnp.concatenate([v[:, :cut] for v in over_y] + [v[:, cut:] for v in over_y], 1)
    weights = jnp.concatenate([ours, swap(ours, c=1)], 0)

    labs = jnp.concatenate([labels, swap(labels, zh=1)], 0)

    def places(order):
        found = []
        for i, kx in enumerate(order):
            for core in (c, 1 - c):
                for kl in range(2):
                    found.append((y ^ ((zl ^ kl) * 2 + core)) * len(order) + i)
        return found

    where = jnp.stack(places(ORDER[:3]) + [x ^ kx for kx in range(4)]).astype(jnp.int32)
    tables = [pair, swap(pair, c=1), near, swap(near, c=1), back, swap(back, c=1)]
    near_k, near_sq, rows = kernel_rows(where, normalized(features), relayed, tables)
    cut = 12 * SLAB
    near_means = lax.dot_general(weights[:, :cut], near_k, (((1,), (1,)), ((), ())), preferred_element_type=F32)
    far, rows, near_means = lax.optimization_barrier((far, rows, near_means))
    where = jnp.stack(places(ORDER[3:])).astype(jnp.int32)
    last = jnp.concatenate(far, 0)
    last_k, last_sq = kernel_rows(where, rows, [], [last, swap(last, c=1)])
    last_means = lax.dot_general(weights[:, cut:], last_k, (((1,), (1,)), ((), ())), preferred_element_type=F32)

    def of_classes(value):
        value = lax.dynamic_slice_in_dim(value, h * half, half, 0)
        return jnp.where(c == 0, value, jnp.concatenate([value[quarter:], value[:quarter]]))[:, None]

    variance, rate = of_classes(class_variance), of_classes(class_rate)
    class_ids = (x * 2 + zl) * all_local + of_classes(jnp.arange(all_local, dtype=jnp.int32))
    means = near_means + last_means
    spread = jnp.sqrt(means * means + variance)
    ratio = rate * jnp.exp(-(means + spread) * 0.5) / (1.0 + jnp.exp(-spread))
    total = jnp.sum(ratio, axis=0).reshape(2, 4, 128)
    turn = total[::-1]
    total = total + swap(total, zl=1) + (swap(turn, zh=1) + swap(turn, zh=1, zl=1))
    total = (total + swap(total, x=2)) + (swap(total, x=1) + swap(total, x=3))
    total = total.reshape(1, -1)
    all_classes = all_local * 8
    intensity = (1.0 + total) / (1.0 + 0.5 * all_classes)
    expected = intensity * ratio
    onehot = (class_ids == labs[None, :]).astype(F32)
    first_weight = ((onehot - expected) * 0.5).astype(BF)
    second_weight = ((onehot + expected) * jnp.tanh(spread * 0.5) / (2.0 * spread)).astype(BF)

    sums = []
    for left, pieces in ((first_weight, (near_k, last_k)), (second_weight, (near_sq, last_sq))):
        keep, give = left[:quarter], left[quarter:]
        theirs = [swap(jnp.dot(give, p, preferred_element_type=F32).astype(BF), c=1) for p in pieces]
        sums.append(([jnp.dot(keep, p, preferred_element_type=F32) for p in pieces], theirs))

    def chunk(which, ky):
        parts = []
        for kept, came in zip(*sums[which]):
            size = kept.shape[1] // 4
            at = slice(ky * size, (ky + 1) * size)
            parts.append(kept[:, at] + came[:, at].astype(F32))
        return jnp.concatenate(parts, 1)

    def over_rows(which, came):
        near, back, far = (value.astype(F32) for value in came)
        return ((chunk(which, 0) + far) + (near + back)).T

    def slab_of(value, kz):
        kx = x ^ zh ^ kz
        return lax.dynamic_slice_in_dim(value, (kx ^ (kx // 2)) * SLAB, SLAB, 0)

    def outgoing(own):
        middle = lax.reduce_precision(jnp.mean(own, axis=0, keepdims=True), 8, 7)
        rest = (own - middle).astype(BF)
        tail = jnp.broadcast_to(middle.astype(BF), (16, quarter))
        return [jnp.concatenate([slab_of(rest, kz), tail], 0) for kz in (2, 1, 3)]

    def total_of(own, got):
        got = [value[:SLAB].astype(F32) + value[SLAB : SLAB + 1].astype(F32) for value in got]
        return jnp.stack([slab_of(own, 0) + got[0], got[1] + got[2]], 1)

    came = [[swap(chunk(0, ky).astype(BF), y=ky) for ky in (1, 3, 2)], [swap(chunk(1, ky).astype(BF), y=ky) for ky in (1, 3)]]
    far, came[0][0] = lax.optimization_barrier((chunk(1, 2).astype(BF), came[0][0]))
    came[1].append(swap(far, y=2))
    own = over_rows(0, came[0])
    send = lax.optimization_barrier(outgoing(own))
    got = [swap(send[0], zh=2), swap(send[1], zh=1)]
    send[2], came[1][0] = lax.optimization_barrier((send[2], came[1][0]))
    got.append(swap(send[2], zh=3))
    came[1], got = lax.optimization_barrier((came[1], got))
    first = total_of(own, got)
    own = over_rows(1, came[1])
    send = lax.optimization_barrier(outgoing(own))
    got = lax.optimization_barrier([swap(value, zh=kz) for value, kz in zip(send, (2, 1, 3))])
    second = total_of(own, got)

    summed = jnp.stack([first, second]) * (1.0 / (512 * 32))
    mine = lax.dynamic_slice_in_dim(summed, c * 64, 64, 1)
    theirs = swap(lax.dynamic_slice_in_dim(summed, (1 - c) * 64, 64, 1), c=1)
    both = jnp.where(c == 0, jnp.stack([mine, theirs], 3), jnp.stack([theirs, mine], 3))
    both = jnp.where(h == 0, both, both[:, :, ::-1])
    out = both.reshape(2, 64, all_local)
    return out[0], out[1]


def solution(mesh):
    parts = Mesh(mesh.devices.reshape(tuple(SIZE.values())), AXES)
    dp, cls = ("zh", "y", "c"), ("x", "zl")
    in_specs = (P(dp, None), P(dp), P(cls, None), P(dp, cls), P(cls), P(cls))
    out_specs = (P(dp, cls), P(dp, cls))
    return jax.shard_map(body, mesh=parts, in_specs=in_specs, out_specs=out_specs, check_vma=False)
```

```python
import jax
import jax.numpy as jnp
from jax import lax
from jax.experimental import pallas as pl
from jax.experimental.pallas import tpu as pltpu
from jax.sharding import Mesh, PartitionSpec as P

SIZE = {"g": 2, "h": 2, "y": 4, "c": 2, "x": 4, "zl": 2}
AXES = tuple(SIZE)
BF = jnp.bfloat16
F32 = jnp.float32
SLAB = 128
ORDER = (0, 1, 3, 2)
PART = 128


def swap(value, zh=0, **masks):
    if zh:
        masks = dict(masks, g=zh // 2, h=zh % 2)
    masks = {a: m for a, m in masks.items() if m}
    names = tuple(a for a in AXES if a in masks)
    pairs, count = [], 1
    for a in names:
        count *= SIZE[a]
    for i in range(count):
        left, at = i, {}
        for a in reversed(names):
            at[a] = left % SIZE[a]
            left //= SIZE[a]
        j = 0
        for a in names:
            j = j * SIZE[a] + (at[a] ^ masks[a])
        pairs.append((i, j))
    return lax.ppermute(value, names, pairs)


def normalized(rows):
    values = rows.astype(F32)
    scale = lax.rsqrt(jnp.mean(values * values, axis=-1, keepdims=True) + 1e-06)
    return (values * scale).astype(BF)


def kernel_rows(places, rows, relayed, tables):
    width = rows.shape[1]
    own = rows.shape[0]
    count = 2 * own if relayed else own
    many = len(tables)
    step = 256
    factor = 1.0 / float(width) ** 0.5

    def body(*refs):
        place, row_ref, refs = refs[0], refs[1], refs[2:]
        relay_refs, table_refs, refs = refs[: len(relayed)], refs[len(relayed) :][:many], refs[len(relayed) + many :]
        out, out_sq = refs[:2]
        held = row_ref
        if relayed:
            held = refs[2]
            held[pl.ds(pl.multiple_of(place[2 * many + 4] * own, own), own)] = row_ref[...]
            for kx in range(4):
                at = pl.multiple_of(place[2 * many + kx] * PART, PART)
                held[pl.ds(at, PART)] = relay_refs[kx][...]

        @pl.loop(0, count // step)
        def _(i):
            block = pl.ds(pl.multiple_of(i * step, step), step)
            left = held[block]
            for n in range(many):
                dots = lax.dot_general(
                    left, table_refs[n][...], (((1,), (1,)), ((), ())), preferred_element_type=F32
                )
                value = jnp.exp(dots * factor).astype(BF)
                wide = value.astype(F32)
                square = (wide * wide).astype(BF)
                for kl in range(2):
                    to = pl.ds(pl.multiple_of(place[n * 2 + kl] * SLAB, SLAB), SLAB)
                    out[block, to] = value[:, kl * SLAB : (kl + 1) * SLAB]
                    out_sq[block, to] = square[:, kl * SLAB : (kl + 1) * SLAB]

    vmem = pl.BlockSpec(memory_space=pltpu.VMEM)
    shape = jax.ShapeDtypeStruct((count, 2 * many * SLAB), BF)
    given = [places, rows, *relayed, *tables]
    return pl.pallas_call(
        body,
        out_shape=(shape, shape) + ((jax.ShapeDtypeStruct((count, width), BF),) if relayed else ()),
        in_specs=[pl.BlockSpec(memory_space=pltpu.SMEM)] + [vmem] * (len(given) - 1),
        out_specs=(vmem, vmem) + ((vmem,) if relayed else ()),
        compiler_params=pltpu.CompilerParams(vmem_limit_bytes=40 << 20),
        cost_estimate=pl.CostEstimate(
            flops=2 * count * 2 * many * SLAB * width,
            bytes_accessed=count * 2 * many * SLAB * 4,
            transcendentals=count * 2 * many * SLAB,
        ),
        name="kernel_rows",
    )(*given)


def body(features, labels, inducing, mean_weights, class_variance, class_rate):
    g, h, y, c, x, zl = (lax.axis_index(a) for a in AXES)
    zh = 2 * g + h
    all_local = mean_weights.shape[1]
    half = all_local // 2
    quarter = half // 2

    mine = normalized(lax.dynamic_slice_in_dim(inducing, c * SLAB, SLAB, 0))
    relay = normalized(lax.dynamic_slice_in_dim(features, x * PART, PART, 0))
    mine, relay, mean_weights = lax.optimization_barrier((mine, relay, mean_weights))
    relay = swap(relay, zh=1)
    pair = jnp.concatenate([mine, swap(mine, zl=1)], 0)

    local = mean_weights.T.reshape(2, 2, quarter, -1)
    keep = lax.dynamic_index_in_dim(local, c, 1, False)
    give = lax.dynamic_index_in_dim(local, 1 - c, 1, False)
    got = swap(give, c=1)
    block = jnp.where(c == 0, jnp.concatenate([keep, got], 2), jnp.concatenate([got, keep], 2))
    same = lax.dynamic_index_in_dim(block, h, 0, False)
    other = lax.dynamic_index_in_dim(block, 1 - h, 0, False)
    (same, other), relay, pair = lax.optimization_barrier(((same, other), relay, pair))
    over_z = jnp.stack([same, swap(other, zh=1), swap(same, zh=2), swap(other, zh=3)])

    pack = jnp.concatenate([pair, relay], 0)
    near, back = swap(pack, x=1), swap(pack, x=3)
    over_z = jnp.concatenate([lax.dynamic_index_in_dim(over_z, zh ^ x ^ kx, 0, False) for kx in ORDER], 1)
    over_z, pack = lax.optimization_barrier((over_z, pack))
    over_y = [over_z, swap(over_z, y=1), swap(over_z, y=2), swap(over_z, y=3)]
    relay_far, near, back, over_y[1], over_y[3] = lax.optimization_barrier(
        (swap(relay, x=2), near, back, over_y[1], over_y[3])
    )
    relayed = [relay, near[2 * SLAB :], relay_far, back[2 * SLAB :]]
    near, back = near[: 2 * SLAB], back[: 2 * SLAB]
    far = [swap(near[:SLAB], x=3), swap(back[SLAB:], x=1)]

    labs = swap(labels, zh=1)
    labs = jnp.where(h == 0, jnp.concatenate([labels, labs]), jnp.concatenate([labs, labels]))

    def places(order):
        found = []
        for i, kx in enumerate(order):
            for core in (c, 1 - c):
                for kl in range(2):
                    found.append((y ^ ((zl ^ kl) * 2 + core)) * len(order) + i)
        return found

    where = places(ORDER[:3]) + [(1 - h) * 4 + (x ^ kx) for kx in range(4)] + [h]
    where = jnp.stack(where).astype(jnp.int32)
    tables = [pair, swap(pair, c=1), near, swap(near, c=1), back, swap(back, c=1)]
    near_k, near_sq, rows = kernel_rows(where, normalized(features), relayed, tables)
    rows, over_y, far = lax.optimization_barrier((rows, over_y, far))
    cut = 3 * SLAB
    ours = jnp.concatenate([v[:, :cut] for v in over_y] + [v[:, cut:] for v in over_y], 1)
    weights = jnp.concatenate([ours, swap(ours, c=1)], 0)
    where = jnp.stack(places(ORDER[3:])).astype(jnp.int32)
    last = jnp.concatenate(far, 0)
    last_k, last_sq = kernel_rows(where, rows, [], [last, swap(last, c=1)])
    cut = 12 * SLAB
    near_means = lax.dot_general(weights[:, :cut], near_k, (((1,), (1,)), ((), ())), preferred_element_type=F32)
    last_means = lax.dot_general(weights[:, cut:], last_k, (((1,), (1,)), ((), ())), preferred_element_type=F32)

    def of_classes(value):
        value = lax.dynamic_slice_in_dim(value, h * half, half, 0)
        return jnp.where(c == 0, value, jnp.concatenate([value[quarter:], value[:quarter]]))[:, None]

    variance, rate = of_classes(class_variance), of_classes(class_rate)
    class_ids = (x * 2 + zl) * all_local + of_classes(jnp.arange(all_local, dtype=jnp.int32))
    means = near_means + last_means
    square = means * means + variance
    inverse = lax.rsqrt(square)
    spread = square * inverse
    small = jnp.exp(-spread)
    share = 1.0 / (1.0 + small)
    ratio = rate * jnp.exp(-(means + spread) * 0.5) * share
    slope = (1.0 - small) * share * (0.5 * inverse)
    total = jnp.sum(ratio, axis=0).reshape(1, 8, 128)
    total = jnp.sum(lax.all_to_all(jnp.tile(total, (16, 1, 1)), ("h", "x", "zl"), 0, 0, tiled=True), axis=0)
    total = total.reshape(1, -1)
    all_classes = all_local * 8
    intensity = (1.0 + total) / (1.0 + 0.5 * all_classes)
    expected = intensity * ratio
    onehot = (class_ids == labs[None, :]).astype(F32)
    first_weight = ((onehot - expected) * 0.5).astype(BF)
    second_weight = ((onehot + expected) * slope).astype(BF)

    sums = []
    for left, pieces in ((first_weight, (near_k, last_k)), (second_weight, (near_sq, last_sq))):
        keep, give = left[:quarter], left[quarter:]
        theirs = [swap(jnp.dot(give, p, preferred_element_type=F32).astype(BF), c=1) for p in pieces]
        sums.append(([jnp.dot(keep, p, preferred_element_type=F32) for p in pieces], theirs))

    def chunk(which, ky):
        parts = []
        for kept, came in zip(*sums[which]):
            size = kept.shape[1] // 4
            at = slice(ky * size, (ky + 1) * size)
            parts.append(kept[:, at] + came[:, at].astype(F32))
        return jnp.concatenate(parts, 1)

    def over_rows(which, came):
        near, back, far = (value.astype(F32) for value in came)
        return (chunk(which, 0) + far) + (near + back)

    def slab_of(value, kz):
        kx = x ^ zh ^ kz
        return lax.dynamic_slice_in_dim(value, (kx ^ (kx // 2)) * SLAB, SLAB, 1)

    def outgoing(own):
        middle = lax.reduce_precision(jnp.mean(own, axis=1), 8, 7)
        rest = (own - middle[:, None]).astype(BF)
        tail = jnp.pad(middle.astype(BF), (0, 16 * SLAB - quarter)).reshape(16, SLAB)
        return [jnp.concatenate([slab_of(rest, kz), tail], 0) for kz in (2, 1, 3)]

    def incoming(value):
        middle = value[quarter:].reshape(-1)[:quarter]
        return value[:quarter].astype(F32) + middle.astype(F32)[:, None]

    came = [[swap(chunk(0, ky).astype(BF), y=ky) for ky in (1, 3, 2)], [swap(chunk(1, ky).astype(BF), y=ky) for ky in (1, 3)]]
    far, came[0][0] = lax.optimization_barrier((chunk(1, 2).astype(BF), came[0][0]))
    came[1].append(swap(far, y=2))
    own = over_rows(0, came[0])
    send = lax.optimization_barrier(outgoing(own))
    got = [swap(send[0], zh=2), swap(send[1], zh=1)]
    send[2], came[1][0], came[1][1] = lax.optimization_barrier((send[2], came[1][0], came[1][1]))
    got.append(swap(send[2], zh=3))
    came[1], got[0], got[1] = lax.optimization_barrier((came[1], got[0], got[1]))
    early = own, got
    own = over_rows(1, came[1])
    send = lax.optimization_barrier(outgoing(own))
    got = [swap(value, zh=kz) for value, kz in zip(send, (2, 1, 3))]

    def total_of(own, got):
        got = [incoming(value) for value in got]
        return jnp.stack([slab_of(own, 0) + got[0], got[1] + got[2]])

    summed = jnp.stack([total_of(*early), total_of(own, got)]) * (1.0 / (512 * 32))
    summed = summed.transpose(0, 3, 1, 2)
    mine = lax.dynamic_slice_in_dim(summed, c * 64, 64, 1)
    theirs = swap(lax.dynamic_slice_in_dim(summed, (1 - c) * 64, 64, 1), c=1)
    both = jnp.where(c == 0, jnp.stack([mine, theirs], 3), jnp.stack([theirs, mine], 3))
    both = jnp.where(h == 0, both, both[:, :, ::-1])
    out = both.reshape(2, 64, all_local)
    return out[0], out[1]


def solution(mesh):
    parts = Mesh(mesh.devices.reshape(tuple(SIZE.values())), AXES)
    dp, cls = ("g", "h", "y", "c"), ("x", "zl")
    in_specs = (P(dp, None), P(dp), P(cls, None), P(dp, cls), P(cls), P(cls))
    out_specs = (P(dp, cls), P(dp, cls))
    return jax.shard_map(body, mesh=parts, in_specs=in_specs, out_specs=out_specs, check_vma=False)
```

```python
import jax
import jax.numpy as jnp
from jax import lax
from jax.experimental import pallas as pl
from jax.experimental.pallas import tpu as pltpu
from jax.sharding import Mesh, PartitionSpec as P

SIZE = {"g": 2, "h": 2, "y": 4, "c": 2, "x": 4, "zl": 2}
AXES = tuple(SIZE)
BF = jnp.bfloat16
F32 = jnp.float32
SLAB = 128
ORDER = (0, 1, 3, 2)
PART = 128


def swap(value, zh=0, **masks):
    if zh:
        masks = dict(masks, g=zh // 2, h=zh % 2)
    masks = {a: m for a, m in masks.items() if m}
    names = tuple(a for a in AXES if a in masks)
    pairs, count = [], 1
    for a in names:
        count *= SIZE[a]
    for i in range(count):
        left, at = i, {}
        for a in reversed(names):
            at[a] = left % SIZE[a]
            left //= SIZE[a]
        j = 0
        for a in names:
            j = j * SIZE[a] + (at[a] ^ masks[a])
        pairs.append((i, j))
    return lax.ppermute(value, names, pairs)


def normalized(rows):
    values = rows.astype(F32)
    scale = lax.rsqrt(jnp.mean(values * values, axis=-1, keepdims=True) + 1e-06)
    return (values * scale).astype(BF)


def kernel_rows(places, rows, relayed, tables):
    width = rows.shape[1]
    own = rows.shape[0]
    count = 2 * own if relayed else own
    many = len(tables)
    step = 256
    factor = 1.0 / float(width) ** 0.5

    def body(*refs):
        place, row_ref, refs = refs[0], refs[1], refs[2:]
        relay_refs, table_refs, refs = refs[: len(relayed)], refs[len(relayed) :][:many], refs[len(relayed) + many :]
        out, out_sq = refs[:2]
        held = row_ref
        if relayed:
            held = refs[2]
            held[pl.ds(pl.multiple_of(place[2 * many + 4] * own, own), own)] = row_ref[...]
            for kx in range(4):
                at = pl.multiple_of(place[2 * many + kx] * PART, PART)
                held[pl.ds(at, PART)] = relay_refs[kx][...]

        @pl.loop(0, count // step)
        def _(i):
            block = pl.ds(pl.multiple_of(i * step, step), step)
            left = held[block]
            for n in range(many):
                dots = lax.dot_general(
                    left, table_refs[n][...], (((1,), (1,)), ((), ())), preferred_element_type=F32
                )
                value = jnp.exp(dots * factor).astype(BF)
                wide = value.astype(F32)
                square = (wide * wide).astype(BF)
                for kl in range(2):
                    to = pl.ds(pl.multiple_of(place[n * 2 + kl] * SLAB, SLAB), SLAB)
                    out[block, to] = value[:, kl * SLAB : (kl + 1) * SLAB]
                    out_sq[block, to] = square[:, kl * SLAB : (kl + 1) * SLAB]

    vmem = pl.BlockSpec(memory_space=pltpu.VMEM)
    shape = jax.ShapeDtypeStruct((count, 2 * many * SLAB), BF)
    given = [places, rows, *relayed, *tables]
    return pl.pallas_call(
        body,
        out_shape=(shape, shape) + ((jax.ShapeDtypeStruct((count, width), BF),) if relayed else ()),
        in_specs=[pl.BlockSpec(memory_space=pltpu.SMEM)] + [vmem] * (len(given) - 1),
        out_specs=(vmem, vmem) + ((vmem,) if relayed else ()),
        compiler_params=pltpu.CompilerParams(vmem_limit_bytes=40 << 20),
        cost_estimate=pl.CostEstimate(
            flops=2 * count * 2 * many * SLAB * width,
            bytes_accessed=count * 2 * many * SLAB * 4,
            transcendentals=count * 2 * many * SLAB,
        ),
        name="kernel_rows",
    )(*given)


def body(features, labels, inducing, mean_weights, class_variance, class_rate):
    g, h, y, c, x, zl = (lax.axis_index(a) for a in AXES)
    zh = 2 * g + h
    all_local = mean_weights.shape[1]
    half = all_local // 2
    quarter = half // 2

    mine = normalized(lax.dynamic_slice_in_dim(inducing, c * SLAB, SLAB, 0))
    relay = normalized(lax.dynamic_slice_in_dim(features, x * PART, PART, 0))
    mine, relay, mean_weights = lax.optimization_barrier((mine, relay, mean_weights))
    relay = swap(relay, zh=1)
    pair = jnp.concatenate([mine, swap(mine, zl=1)], 0)

    local = mean_weights.T.reshape(2, 2, quarter, -1)
    keep = lax.dynamic_index_in_dim(local, c, 1, False)
    give = lax.dynamic_index_in_dim(local, 1 - c, 1, False)
    got = swap(give, c=1)
    block = jnp.where(c == 0, jnp.concatenate([keep, got], 2), jnp.concatenate([got, keep], 2))
    same = lax.dynamic_index_in_dim(block, h, 0, False)
    other = lax.dynamic_index_in_dim(block, 1 - h, 0, False)
    over_z = jnp.stack([same, swap(other, zh=1), swap(same, zh=2), swap(other, zh=3)])
    over_z = jnp.concatenate([lax.dynamic_index_in_dim(over_z, zh ^ x ^ kx, 0, False) for kx in ORDER], 1)

    pack = jnp.concatenate([pair, relay], 0)
    near, back = swap(pack, x=1), swap(pack, x=3)
    over_z, pack = lax.optimization_barrier((over_z, pack))
    over_y = [over_z, swap(over_z, y=1), None, swap(over_z, y=3)]
    relay_far, near, back, over_y[1], over_y[3], over_z = lax.optimization_barrier(
        (swap(relay, x=2), near, back, over_y[1], over_y[3], over_z)
    )
    over_y[2] = swap(over_z, y=2)
    relayed = [relay, near[2 * SLAB :], relay_far, back[2 * SLAB :]]
    near, back = near[: 2 * SLAB], back[: 2 * SLAB]
    far = [swap(near[:SLAB], x=3), swap(back[SLAB:], x=1)]

    labs = swap(labels, zh=1)
    labs = jnp.where(h == 0, jnp.concatenate([labels, labs]), jnp.concatenate([labs, labels]))

    def places(order):
        found = []
        for i, kx in enumerate(order):
            for core in (c, 1 - c):
                for kl in range(2):
                    found.append((y ^ ((zl ^ kl) * 2 + core)) * len(order) + i)
        return found

    where = places(ORDER[:3]) + [(1 - h) * 4 + (x ^ kx) for kx in range(4)] + [h]
    where = jnp.stack(where).astype(jnp.int32)
    tables = [pair, swap(pair, c=1), near, swap(near, c=1), back, swap(back, c=1)]
    near_k, near_sq, rows = kernel_rows(where, normalized(features), relayed, tables)
    rows, over_y, far = lax.optimization_barrier((rows, over_y, far))
    cut = 3 * SLAB
    ours = jnp.concatenate([v[:, :cut] for v in over_y] + [v[:, cut:] for v in over_y], 1)
    weights = jnp.concatenate([ours, swap(ours, c=1)], 0)
    where = jnp.stack(places(ORDER[3:])).astype(jnp.int32)
    last = jnp.concatenate(far, 0)
    last_k, last_sq = kernel_rows(where, rows, [], [last, swap(last, c=1)])
    cut = 12 * SLAB
    near_means = lax.dot_general(weights[:, :cut], near_k, (((1,), (1,)), ((), ())), preferred_element_type=F32)
    last_means = lax.dot_general(weights[:, cut:], last_k, (((1,), (1,)), ((), ())), preferred_element_type=F32)

    def of_classes(value):
        value = lax.dynamic_slice_in_dim(value, h * half, half, 0)
        return jnp.where(c == 0, value, jnp.concatenate([value[quarter:], value[:quarter]]))[:, None]

    variance, rate = of_classes(class_variance), of_classes(class_rate)
    class_ids = (x * 2 + zl) * all_local + of_classes(jnp.arange(all_local, dtype=jnp.int32))
    means = near_means + last_means
    square = means * means + variance
    inverse = lax.rsqrt(square)
    spread = square * inverse
    small = jnp.exp(-spread)
    share = 1.0 / (1.0 + small)
    ratio = rate * jnp.exp(-(means + spread) * 0.5) * share
    slope = (1.0 - small) * share * (0.5 * inverse)
    total = jnp.sum(ratio, axis=0).reshape(1, 8, 128)
    total = jnp.sum(lax.all_to_all(jnp.tile(total, (16, 1, 1)), ("h", "x", "zl"), 0, 0, tiled=True), axis=0)
    total = total.reshape(1, -1)
    all_classes = all_local * 8
    intensity = (1.0 + total) / (1.0 + 0.5 * all_classes)
    onehot = (class_ids == labs[None, :]).astype(F32)

    def products(left, pieces):
        keep, give = left[:quarter], left[quarter:]
        theirs = [swap(jnp.dot(give, p, preferred_element_type=F32).astype(BF), c=1) for p in pieces]
        return [jnp.dot(keep, p, preferred_element_type=F32) for p in pieces], theirs

    kept, theirs = products(((onehot - intensity * ratio) * 0.5).astype(BF), (near_k, last_k))
    kept, theirs, intensity, ratio, slope = lax.optimization_barrier((kept, theirs, intensity, ratio, slope))
    sums = [(kept, theirs), products(((onehot + intensity * ratio) * slope).astype(BF), (near_sq, last_sq))]

    def chunk(which, ky):
        parts = []
        for kept, came in zip(*sums[which]):
            size = kept.shape[1] // 4
            at = slice(ky * size, (ky + 1) * size)
            parts.append(kept[:, at] + came[:, at].astype(F32))
        return jnp.concatenate(parts, 1)

    def over_rows(which, came):
        near, back, far = (value.astype(F32) for value in came)
        return (chunk(which, 0) + far) + (near + back)

    def slab_of(value, kz):
        kx = x ^ zh ^ kz
        return lax.dynamic_slice_in_dim(value, (kx ^ (kx // 2)) * SLAB, SLAB, 1)

    def outgoing(own):
        middle = lax.reduce_precision(jnp.mean(own, axis=1), 8, 7)
        rest = (own - middle[:, None]).astype(BF)
        tail = jnp.pad(middle.astype(BF), (0, 16 * SLAB - quarter)).reshape(16, SLAB)
        return [jnp.concatenate([slab_of(rest, kz), tail], 0) for kz in (2, 1, 3)]

    def incoming(value):
        middle = value[quarter:].reshape(-1)[:quarter]
        return value[:quarter].astype(F32) + middle.astype(F32)[:, None]

    came = [[swap(chunk(0, ky).astype(BF), y=ky) for ky in (1, 3, 2)], [swap(chunk(1, ky).astype(BF), y=ky) for ky in (1, 3)]]
    far, came[0][0] = lax.optimization_barrier((chunk(1, 2).astype(BF), came[0][0]))
    came[1].append(swap(far, y=2))
    own = over_rows(0, came[0])
    send = lax.optimization_barrier(outgoing(own))
    got = [swap(send[0], zh=2), swap(send[1], zh=1)]
    came[1], got = lax.optimization_barrier((came[1], got))
    early, late, own_early = got, send[2], own
    own = over_rows(1, came[1])
    send = lax.optimization_barrier(outgoing(own))
    both = swap(jnp.concatenate([send[2], late], 0), zh=3)
    early = early + [both[quarter + 16 :]]
    got = [swap(send[0], zh=2), swap(send[1], zh=1), both[: quarter + 16]]

    def total_of(own, got):
        got = [incoming(value) for value in got]
        return jnp.stack([slab_of(own, 0) + got[0], got[1] + got[2]])

    summed = jnp.stack([total_of(own_early, early), total_of(own, got)]) * (1.0 / (512 * 32))
    summed = summed.transpose(0, 3, 1, 2)
    mine = lax.dynamic_slice_in_dim(summed, c * 64, 64, 1)
    theirs = swap(lax.dynamic_slice_in_dim(summed, (1 - c) * 64, 64, 1), c=1)
    both = jnp.where(c == 0, jnp.stack([mine, theirs], 3), jnp.stack([theirs, mine], 3))
    both = jnp.where(h == 0, both, both[:, :, ::-1])
    out = both.reshape(2, 64, all_local)
    return out[0], out[1]


def solution(mesh):
    parts = Mesh(mesh.devices.reshape(tuple(SIZE.values())), AXES)
    dp, cls = ("g", "h", "y", "c"), ("x", "zl")
    in_specs = (P(dp, None), P(dp), P(cls, None), P(dp, cls), P(cls), P(cls))
    out_specs = (P(dp, cls), P(dp, cls))
    return jax.shard_map(body, mesh=parts, in_specs=in_specs, out_specs=out_specs, check_vma=False)
```

```python
import jax
import jax.numpy as jnp
from jax import lax
from jax.experimental import pallas as pl
from jax.experimental.pallas import tpu as pltpu
from jax.sharding import Mesh, PartitionSpec as P

SIZE = {"g": 2, "h": 2, "y": 4, "c": 2, "x": 4, "zl": 2}
AXES = tuple(SIZE)
BF = jnp.bfloat16
F32 = jnp.float32
SLAB = 128
ORDER = (0, 1, 3, 2)
PART = 128


def swap(value, zh=0, **masks):
    if zh:
        masks = dict(masks, g=zh // 2, h=zh % 2)
    masks = {a: m for a, m in masks.items() if m}
    names = tuple(a for a in AXES if a in masks)
    pairs, count = [], 1
    for a in names:
        count *= SIZE[a]
    for i in range(count):
        left, at = i, {}
        for a in reversed(names):
            at[a] = left % SIZE[a]
            left //= SIZE[a]
        j = 0
        for a in names:
            j = j * SIZE[a] + (at[a] ^ masks[a])
        pairs.append((i, j))
    return lax.ppermute(value, names, pairs)


def normalized(rows):
    values = rows.astype(F32)
    scale = lax.rsqrt(jnp.mean(values * values, axis=-1, keepdims=True) + 1e-06)
    return (values * scale).astype(BF)


def vmem_call(body, name, out_shape, given, scratch=(), flops=0, smem=0):
    vmem = pl.BlockSpec(memory_space=pltpu.VMEM)
    moved = sum(v.size * v.dtype.itemsize for v in (*given, *out_shape))
    return pl.pallas_call(
        body,
        out_shape=tuple(out_shape),
        in_specs=[pl.BlockSpec(memory_space=pltpu.SMEM)] * smem + [vmem] * (len(given) - smem),
        out_specs=(vmem,) * len(out_shape),
        scratch_shapes=list(scratch),
        compiler_params=pltpu.CompilerParams(vmem_limit_bytes=48 << 20),
        cost_estimate=pl.CostEstimate(flops=flops, bytes_accessed=moved, transcendentals=0),
        name=name,
    )(*given)


def slab_at(index):
    return pl.ds(pl.multiple_of(index * SLAB, SLAB), SLAB)


def write_rows(left, table, place, first, factor, out, out_sq, block):
    dots = lax.dot_general(left, table, (((1,), (1,)), ((), ())), preferred_element_type=F32)
    value = jnp.exp(dots * factor).astype(BF)
    wide = value.astype(F32)
    square = (wide * wide).astype(BF)
    for kl in range(2):
        to = slab_at(place[first + kl])
        out[block, to] = value[:, kl * SLAB : (kl + 1) * SLAB]
        out_sq[block, to] = square[:, kl * SLAB : (kl + 1) * SLAB]


def near_rows(places, features, relay, relay_far, pair, across, packs, across_packs):
    own, width = features.shape
    factor = 1.0 / float(width) ** 0.5
    step = 512

    def body(place, feature, relay, relay_far, pair, across, near, back, near_a, back_a, out, out_sq, held):
        held[pl.ds(pl.multiple_of(place[16] * own, own), own)] = normalized(feature[...])
        for k, rows in enumerate((relay, near, relay_far, back)):
            at = pl.ds(pl.multiple_of(place[12 + k] * PART, PART), PART)
            held[at] = rows[...] if k % 2 == 0 else rows[2 * SLAB :]
        tables = (pair, across, near, near_a, back, back_a)

        @pl.loop(0, 2 * own // step)
        def _(i):
            block = pl.ds(pl.multiple_of(i * step, step), step)
            for n, table in enumerate(tables):
                write_rows(held[block], table[: 2 * SLAB], place, 2 * n, factor, out, out_sq, block)

    shape = jax.ShapeDtypeStruct((2 * own, 12 * SLAB), BF)
    given = [places, features, relay, relay_far, pair, across, *packs, *across_packs]
    return vmem_call(
        body, "near_rows", (shape, shape, jax.ShapeDtypeStruct((2 * own, width), BF)), given, (), 4 * own * 12 * SLAB * width, 1
    )


def means_of(places, rows, far, far_across, near_k, ours, theirs, variance, rate):
    count, width = rows.shape
    quarter = ours[0].shape[0]
    factor = 1.0 / float(width) ** 0.5
    step, cut, cols = 256, 3 * SLAB, 4 * SLAB

    def body(place, rows, far, far_across, near_k, *refs):
        blocks, (variance, rate, out, out_sq, ratio, slope, total, weights) = refs[:8], refs[8:]
        for k in range(2):
            here = slice(k * quarter, (k + 1) * quarter)
            for ky in range(4):
                block = blocks[4 * k + ky]
                weights[here, ky * cut : (ky + 1) * cut] = block[:, :cut]
                weights[here, 12 * SLAB + ky * SLAB : 12 * SLAB + (ky + 1) * SLAB] = block[:, cut:]

        @pl.loop(0, count // 512)
        def _(i):
            block = pl.ds(pl.multiple_of(i * 512, 512), 512)
            for n, table in enumerate((far, far_across)):
                write_rows(rows[block], table[...], place, 2 * n, factor, out, out_sq, block)

        @pl.loop(0, count // step)
        def _(i):
            block = pl.ds(pl.multiple_of(i * step, step), step)
            transposed = (((1,), (1,)), ((), ()))
            for k in range(2):
                here = slice(k * quarter, (k + 1) * quarter)
                means = lax.dot_general(
                    weights[here, : 12 * SLAB], near_k[block], transposed, preferred_element_type=F32
                ) + lax.dot_general(weights[here, 12 * SLAB :], out[block], transposed, preferred_element_type=F32)
                square = means * means + variance[here]
                inverse = lax.rsqrt(square)
                spread = square * inverse
                small = jnp.exp(-spread)
                share = 1.0 / (1.0 + small)
                value = rate[here] * jnp.exp(-(means + spread) * 0.5) * share
                ratio[here, block] = value
                slope[here, block] = (1.0 - small) * share * (0.5 * inverse)
                part = jnp.sum(value, axis=0, keepdims=True)
                total[:, block] = part if k == 0 else total[:, block] + part

    wide = jax.ShapeDtypeStruct((2 * quarter, count), F32)
    last = jax.ShapeDtypeStruct((count, 4 * SLAB), BF)
    given = [places, rows, far, far_across, near_k, *ours, *theirs, variance, rate]
    return vmem_call(
        body,
        "means",
        (last, last, wide, wide, jax.ShapeDtypeStruct((1, count), F32)),
        given,
        [pltpu.VMEM((2 * quarter, 4 * cols), BF)],
        2 * count * 16 * SLAB * 2 * quarter,
        1,
    )


def statistic(which, ratio, slope, intensity, labels, ids, near, last):
    quarter, count = ratio.shape[0] // 2, ratio.shape[1]
    step = 2 * SLAB

    def body(ratio, slope, intensity, labels, ids, near, last, keep, give, weight):
        for k in range(4):
            here = slice(k * quarter // 2, (k + 1) * quarter // 2)
            hot = (ids[here] == labels[...]).astype(F32)
            expected = intensity[...] * ratio[here]
            value = (hot - expected) * 0.5 if which == 0 else (hot + expected) * slope[here]
            weight[here] = value.astype(BF)

        for source, per in ((near, 3), (last, 1)):

            @pl.loop(0, source.shape[1] // step)
            def _(j):
                block = pl.ds(pl.multiple_of(j * step, step), step)
                sums = jnp.dot(weight[...], source[:, block], preferred_element_type=F32)
                for k in range(2):
                    slab = 2 * j + k
                    ky = slab // per
                    to = slab_at(ky * 4 + (slab - ky * per if per == 3 else 3))
                    part = sums[:, k * SLAB : (k + 1) * SLAB]
                    keep[:, to] = part[:quarter]
                    give[:, to] = part[quarter:].astype(BF)

    shape = (quarter, 16 * SLAB)
    given = [ratio, slope, intensity, labels, ids, near, last]
    return vmem_call(
        body,
        "statistic",
        (jax.ShapeDtypeStruct(shape, F32), jax.ShapeDtypeStruct(shape, BF)),
        given,
        [pltpu.VMEM(ratio.shape, BF)],
        2 * count * 16 * SLAB * 2 * quarter,
    )


def body(features, labels, inducing, mean_weights, class_variance, class_rate):
    g, h, y, c, x, zl = (lax.axis_index(a) for a in AXES)
    zh = 2 * g + h
    all_local = mean_weights.shape[1]
    half = all_local // 2
    quarter = half // 2

    mine = normalized(lax.dynamic_slice_in_dim(inducing, c * SLAB, SLAB, 0))
    relay = normalized(lax.dynamic_slice_in_dim(features, x * PART, PART, 0))
    mine, relay, mean_weights = lax.optimization_barrier((mine, relay, mean_weights))
    relay = swap(relay, zh=1)
    labs = swap(labels, zh=1)
    pair = jnp.concatenate([mine, swap(mine, zl=1)], 0)

    local = mean_weights.T.reshape(2, 2, quarter, -1)
    keep = lax.dynamic_index_in_dim(local, c, 1, False)
    give = lax.dynamic_index_in_dim(local, 1 - c, 1, False)
    got = swap(give, c=1)
    block = jnp.where(c == 0, jnp.concatenate([keep, got], 2), jnp.concatenate([got, keep], 2))
    same = lax.dynamic_index_in_dim(block, h, 0, False)
    other = lax.dynamic_index_in_dim(block, 1 - h, 0, False)
    over_z = jnp.stack([same, swap(other, zh=1), swap(same, zh=2), swap(other, zh=3)])
    over_z = jnp.concatenate([lax.dynamic_index_in_dim(over_z, zh ^ x ^ kx, 0, False) for kx in ORDER], 1)

    pack = jnp.concatenate([pair, relay], 0)
    near, back = swap(pack, x=1), swap(pack, x=3)
    over_z, pack, labs = lax.optimization_barrier((over_z, pack, labs))
    over_y = [over_z, swap(over_z, y=1), None, swap(over_z, y=3)]
    relay_far, near, back, pair, over_z, over_y[1], over_y[3] = lax.optimization_barrier(
        (swap(relay, x=2), near, back, pair, over_z, over_y[1], over_y[3])
    )
    over_y[2] = swap(over_z, y=2)
    far = swap(pair, x=2)

    def places(order):
        found = []
        for i, kx in enumerate(order):
            for core in (c, 1 - c):
                for kl in range(2):
                    found.append((y ^ ((zl ^ kl) * 2 + core)) * len(order) + i)
        return found

    where = places(ORDER[:3]) + [(1 - h) * 4 + (x ^ kx) for kx in range(4)] + [h]
    where = jnp.stack(where).astype(jnp.int32)
    across = (swap(near, c=1), swap(back, c=1))
    near_k, near_sq, rows = near_rows(where, features, relay, relay_far, pair, swap(pair, c=1), (near, back), across)
    far, rows = lax.optimization_barrier((far, rows))

    def of_classes(value):
        value = lax.dynamic_slice_in_dim(value, h * half, half, 0)
        return jnp.where(c == 0, value, jnp.concatenate([value[quarter:], value[:quarter]]))[:, None]

    ids = (x * 2 + zl) * all_local + of_classes(jnp.arange(all_local, dtype=jnp.int32))
    labs = jnp.where(h == 0, jnp.concatenate([labels, labs]), jnp.concatenate([labs, labels]))[None, :]
    where = jnp.stack(places(ORDER[3:])).astype(jnp.int32)
    last_k, last_sq, ratio, slope, total = means_of(
        where, rows, far, swap(far, c=1), near_k, over_y, [swap(v, c=1) for v in over_y],
        of_classes(class_variance), of_classes(class_rate),
    )
    total = jnp.tile(total.reshape(1, 8, 128), (16, 1, 1))
    total = jnp.sum(lax.all_to_all(total, ("h", "x", "zl"), 0, 0, tiled=True), axis=0).reshape(1, -1)
    all_classes = all_local * 8
    intensity = (1.0 + total) / (1.0 + 0.5 * all_classes)

    sums = []
    for which, (near_part, last_part) in enumerate(((near_k, last_k), (near_sq, last_sq))):
        kept, give = statistic(which, ratio, slope, intensity, labs, ids, near_part, last_part)
        sums.append((kept, swap(give, c=1)))

    def chunk(which, ky):
        at = slice(ky * 512, (ky + 1) * 512)
        return sums[which][0][:, at] + sums[which][1][:, at].astype(F32)

    def over_rows(which, came):
        near, back, far = (value.astype(F32) for value in came)
        return (chunk(which, 0) + far) + (near + back)

    def slab_of(value, kz):
        kx = x ^ zh ^ kz
        return lax.dynamic_slice_in_dim(value, (kx ^ (kx // 2)) * SLAB, SLAB, 1)

    def outgoing(own):
        middle = lax.reduce_precision(jnp.mean(own, axis=1), 8, 7)
        rest = (own - middle[:, None]).astype(BF)
        tail = jnp.pad(middle.astype(BF), (0, 16 * SLAB - quarter)).reshape(16, SLAB)
        return [jnp.concatenate([slab_of(rest, kz), tail], 0) for kz in (2, 1, 3)]

    def incoming(value):
        middle = value[quarter:].reshape(-1)[:quarter]
        return value[:quarter].astype(F32) + middle.astype(F32)[:, None]

    came = [[swap(chunk(0, ky).astype(BF), y=ky) for ky in (1, 3, 2)], [swap(chunk(1, ky).astype(BF), y=ky) for ky in (1, 3)]]
    far, came[0][0] = lax.optimization_barrier((chunk(1, 2).astype(BF), came[0][0]))
    came[1].append(swap(far, y=2))
    own = over_rows(0, came[0])
    send = lax.optimization_barrier(outgoing(own))
    got = [swap(send[0], zh=2), swap(send[1], zh=1)]
    came[1], got = lax.optimization_barrier((came[1], got))
    early, late, own_early = got, send[2], own
    own = over_rows(1, came[1])
    send = lax.optimization_barrier(outgoing(own))
    both = swap(jnp.concatenate([send[2], late], 0), zh=3)
    early = early + [both[quarter + 16 :]]
    got = [swap(send[0], zh=2), swap(send[1], zh=1), both[: quarter + 16]]

    def total_of(own, got):
        got = [incoming(value) for value in got]
        return jnp.stack([slab_of(own, 0) + got[0], got[1] + got[2]])

    summed = jnp.stack([total_of(own_early, early), total_of(own, got)]) * (1.0 / (512 * 32))
    summed = summed.transpose(0, 3, 1, 2)
    mine = lax.dynamic_slice_in_dim(summed, c * 64, 64, 1)
    theirs = swap(lax.dynamic_slice_in_dim(summed, (1 - c) * 64, 64, 1), c=1)
    both = jnp.where(c == 0, jnp.stack([mine, theirs], 3), jnp.stack([theirs, mine], 3))
    both = jnp.where(h == 0, both, both[:, :, ::-1])
    out = both.reshape(2, 64, all_local)
    return out[0], out[1]


def solution(mesh):
    parts = Mesh(mesh.devices.reshape(tuple(SIZE.values())), AXES)
    dp, cls = ("g", "h", "y", "c"), ("x", "zl")
    in_specs = (P(dp, None), P(dp), P(cls, None), P(dp, cls), P(cls), P(cls))
    out_specs = (P(dp, cls), P(dp, cls))
    return jax.shard_map(body, mesh=parts, in_specs=in_specs, out_specs=out_specs, check_vma=False)
```

```python
import jax
import jax.numpy as jnp
from jax import lax
from jax.experimental import pallas as pl
from jax.experimental.pallas import tpu as pltpu
from jax.sharding import Mesh, PartitionSpec as P

SIZE = {"g": 2, "h": 2, "y": 4, "c": 2, "x": 4, "zl": 2}
AXES = tuple(SIZE)
BF = jnp.bfloat16
F32 = jnp.float32
SLAB = 128
ORDER = (0, 1, 3, 2)
PART = 128


def swap(value, zh=0, **masks):
    if zh:
        masks = dict(masks, g=zh // 2, h=zh % 2)
    masks = {a: m for a, m in masks.items() if m}
    names = tuple(a for a in AXES if a in masks)
    pairs, count = [], 1
    for a in names:
        count *= SIZE[a]
    for i in range(count):
        left, at = i, {}
        for a in reversed(names):
            at[a] = left % SIZE[a]
            left //= SIZE[a]
        j = 0
        for a in names:
            j = j * SIZE[a] + (at[a] ^ masks[a])
        pairs.append((i, j))
    return lax.ppermute(value, names, pairs)


def normalized(rows):
    values = rows.astype(F32)
    scale = lax.rsqrt(jnp.mean(values * values, axis=-1, keepdims=True) + 1e-06)
    return (values * scale).astype(BF)


def unit_slabs(at, points, features):
    def body(at, points, features, out, out_rows):
        out[...] = normalized(points[...])
        out_rows[...] = normalized(features[...])

    spec = lambda k: pl.BlockSpec((SLAB, points.shape[1]), lambda i, at: (at[k], 0))
    kept = pl.BlockSpec((SLAB, points.shape[1]), lambda i, at: (0, 0))
    shape = jax.ShapeDtypeStruct((SLAB, points.shape[1]), BF)
    grid = pltpu.PrefetchScalarGridSpec(
        num_scalar_prefetch=1, grid=(1,), in_specs=[spec(0), spec(1)], out_specs=[kept, kept]
    )
    return pl.pallas_call(body, grid_spec=grid, out_shape=[shape, shape], name="unit_slabs")(at, points, features)


def whole(value):
    return pl.BlockSpec(value.shape, lambda i: (0,) * value.ndim, pipeline_mode=pl.Buffered(1))


def stepped(body, name, steps, given, in_specs, out_shape, out_specs, scratch, flops):
    moved = 4 * sum(v.size for v in given)
    return pl.pallas_call(
        body,
        grid=(steps,),
        out_shape=out_shape,
        in_specs=in_specs,
        out_specs=out_specs,
        scratch_shapes=scratch,
        compiler_params=pltpu.CompilerParams(vmem_limit_bytes=48 << 20),
        cost_estimate=pl.CostEstimate(flops=flops, bytes_accessed=moved, transcendentals=0),
        name=name,
    )(*given)


def write_rows(left, table, place, first, factor, out, out_sq):
    dots = lax.dot_general(left, table, (((1,), (1,)), ((), ())), preferred_element_type=F32)
    value = jnp.exp(dots * factor).astype(BF)
    square = value * value
    for kl in range(2):
        to = pl.ds(pl.multiple_of(place[first + kl] * SLAB, SLAB), SLAB)
        out[:, to] = value[:, kl * SLAB : (kl + 1) * SLAB]
        out_sq[:, to] = square[:, kl * SLAB : (kl + 1) * SLAB]


def near_rows(places, features, relay, relay_far, pair, across, packs, across_packs):
    own, width = features.shape
    factor = 1.0 / float(width) ** 0.5
    step = 256

    def body(place, feature, relay, relay_far, pair, across, near, back, near_a, back_a, out, out_sq, rows_out, held):
        i = pl.program_id(0)

        @pl.when(i == 0)
        def _():
            held[pl.ds(pl.multiple_of(place[16] * own, own), own)] = normalized(feature[...])
            for k, rows in enumerate((relay, near, relay_far, back)):
                at = pl.ds(pl.multiple_of(place[12 + k] * PART, PART), PART)
                held[at] = rows[...] if k % 2 == 0 else rows[2 * SLAB :]

        left = held[pl.ds(pl.multiple_of(i * step, step), step)]
        rows_out[...] = left
        for n, table in enumerate((pair, across, near, near_a, back, back_a)):
            write_rows(left, table[: 2 * SLAB], place, 2 * n, factor, out, out_sq)

    given = [places, features, relay, relay_far, pair, across, *packs, *across_packs]
    shapes = [jax.ShapeDtypeStruct((2 * own, n), BF) for n in (12 * SLAB, 12 * SLAB, width)]
    return stepped(
        body,
        "near_rows",
        2 * own // step,
        given,
        [pl.BlockSpec(memory_space=pltpu.SMEM)] + [whole(v) for v in given[1:]],
        shapes,
        [pl.BlockSpec((step, s.shape[1]), lambda i: (i, 0)) for s in shapes],
        [pltpu.VMEM((2 * own, width), BF)],
        4 * own * 12 * SLAB * width,
    )


def means_of(places, rows, far, far_across, near_k, ours, theirs, variance, rate):
    count, width = rows.shape
    quarter = ours[0].shape[0]
    factor = 1.0 / float(width) ** 0.5
    step, cut = 256, 3 * SLAB

    def body(place, rows, far, far_across, near_k, *refs):
        blocks, (variance, rate, out, out_sq, ratio, slope, total, weights, held) = refs[:8], refs[8:]

        @pl.when(pl.program_id(0) == 0)
        def _():
            for k in range(2):
                here = slice(k * quarter, (k + 1) * quarter)
                for ky in range(4):
                    block = blocks[4 * k + ky]
                    weights[here, ky * cut : (ky + 1) * cut] = block[:, :cut]
                    weights[here, 12 * SLAB + ky * SLAB : 12 * SLAB + (ky + 1) * SLAB] = block[:, cut:]

        for n, table in enumerate((far, far_across)):
            write_rows(rows[...], table[...], place, 2 * n, factor, out, out_sq)
        transposed = (((1,), (1,)), ((), ()))
        held[...] = lax.dot_general(
            weights[:, : 12 * SLAB], near_k[...], transposed, preferred_element_type=F32
        ) + lax.dot_general(weights[:, 12 * SLAB :], out[...], transposed, preferred_element_type=F32)
        part = jnp.zeros((1, step), F32)
        for k in range(4):
            here = slice(k * quarter // 2, (k + 1) * quarter // 2)
            means = held[here]
            square = means * means + variance[here]
            inverse = lax.rsqrt(square)
            spread = square * inverse
            small = jnp.exp(-spread)
            share = 1.0 / (1.0 + small)
            value = rate[here] * jnp.exp(-(means + spread) * 0.5) * share
            ratio[here] = value
            slope[here] = (1.0 - small) * share * (0.5 * inverse)
            part += jnp.sum(value, axis=0, keepdims=True)
        total[...] = part

    given = [places, rows, far, far_across, near_k, *ours, *theirs, variance, rate]
    wide = jax.ShapeDtypeStruct((2 * quarter, count), F32)
    last = jax.ShapeDtypeStruct((count, 4 * SLAB), BF)
    by_rows = lambda v: pl.BlockSpec((step, v.shape[1]), lambda i: (i, 0))
    by_columns = lambda v: pl.BlockSpec((v.shape[0], step), lambda i: (0, i))
    total = jax.ShapeDtypeStruct((1, count), F32)
    return stepped(
        body,
        "means",
        count // step,
        given,
        [pl.BlockSpec(memory_space=pltpu.SMEM), by_rows(rows), whole(far), whole(far_across), by_rows(near_k)]
        + [whole(v) for v in given[5:]],
        [pltpu.HBM(last.shape, BF), pltpu.HBM(last.shape, BF), wide, wide, total],
        [by_rows(last), by_rows(last), by_columns(wide), by_columns(wide), by_columns(total)],
        [pltpu.VMEM((2 * quarter, 16 * SLAB), BF), pltpu.VMEM((2 * quarter, step), F32)],
        2 * count * 16 * SLAB * 2 * quarter,
    )


def statistic(ratio, slope, intensity, labels, ids, near, last):
    quarter, count = ratio.shape[0] // 2, ratio.shape[1]
    steps = 4

    def body(*refs):
        ratio, slope = refs[0], refs[1] if slopes else None
        intensity, labels, ids, near, last, keep, give, weight, joint = refs[1 + len(slopes) :]

        @pl.when(pl.program_id(0) == 0)
        def _():
            for k in range(4):
                here = slice(k * quarter // 2, (k + 1) * quarter // 2)
                hot = (ids[here] == labels[...]).astype(F32)
                expected = intensity[...] * ratio[here]
                value = (hot - expected) * 0.5 if slope is None else (hot + expected) * slope[here]
                weight[here] = value.astype(BF)

        joint[:, : 3 * SLAB] = near[...]
        joint[:, 3 * SLAB :] = last[...]
        sums = jnp.dot(weight[...], joint[...], preferred_element_type=F32)
        keep[...] = sums[:quarter]
        give[...] = sums[quarter:].astype(BF)

    slopes = [] if slope is None else [slope]
    given = [ratio, *slopes, intensity, labels, ids, near, last]
    block = lambda rows, cols: pl.BlockSpec((rows, cols), lambda i: (0, i))
    return stepped(
        body,
        "statistic",
        steps,
        given,
        [whole(v) for v in given[:-2]] + [block(count, 3 * SLAB), block(count, SLAB)],
        [jax.ShapeDtypeStruct((quarter, 16 * SLAB), F32), jax.ShapeDtypeStruct((quarter, 16 * SLAB), BF)],
        [block(quarter, 4 * SLAB), block(quarter, 4 * SLAB)],
        [pltpu.VMEM(ratio.shape, BF), pltpu.VMEM((count, 4 * SLAB), BF)],
        2 * count * 16 * SLAB * 2 * quarter,
    )


def body(features, labels, inducing, mean_weights, class_variance, class_rate):
    g, h, y, c, x, zl = (lax.axis_index(a) for a in AXES)
    zh = 2 * g + h
    all_local = mean_weights.shape[1]
    half = all_local // 2
    quarter = half // 2

    mine, relay = unit_slabs(jnp.stack([c, x]).astype(jnp.int32), inducing, features)
    mine, relay, mean_weights = lax.optimization_barrier((mine, relay, mean_weights))
    relay = swap(relay, zh=1)
    labs = swap(labels, zh=1)
    pair = jnp.concatenate([mine, swap(mine, zl=1)], 0)

    local = mean_weights.T.reshape(2, 2, quarter, -1)
    keep = lax.dynamic_index_in_dim(local, c, 1, False)
    give = lax.dynamic_index_in_dim(local, 1 - c, 1, False)
    got = swap(give, c=1)
    block = jnp.where(c == 0, jnp.concatenate([keep, got], 2), jnp.concatenate([got, keep], 2))
    same = lax.dynamic_index_in_dim(block, h, 0, False)
    other = lax.dynamic_index_in_dim(block, 1 - h, 0, False)
    over_z = jnp.stack([same, swap(other, zh=1), swap(same, zh=2), swap(other, zh=3)])
    over_z = jnp.concatenate([lax.dynamic_index_in_dim(over_z, zh ^ x ^ kx, 0, False) for kx in ORDER], 1)

    pack = jnp.concatenate([pair, relay], 0)
    near, back = swap(pack, x=1), swap(pack, x=3)
    over_z, pack = lax.optimization_barrier((over_z, pack))
    over_y = [over_z, swap(over_z, y=1), None, swap(over_z, y=3)]
    relay_far, near, back, pair, labs, over_z, over_y[1], over_y[3] = lax.optimization_barrier(
        (swap(relay, x=2), near, back, pair, labs, over_z, over_y[1], over_y[3])
    )
    over_y[2] = swap(over_z, y=2)
    far = swap(pair, x=2)

    def places(order):
        found = []
        for i, kx in enumerate(order):
            for core in (c, 1 - c):
                for kl in range(2):
                    found.append((y ^ ((zl ^ kl) * 2 + core)) * len(order) + i)
        return found

    where = places(ORDER[:3]) + [(1 - h) * 4 + (x ^ kx) for kx in range(4)] + [h]
    where = jnp.stack(where).astype(jnp.int32)
    across = (swap(near, c=1), swap(back, c=1))
    near_k, near_sq, rows = near_rows(where, features, relay, relay_far, pair, swap(pair, c=1), (near, back), across)
    far, rows = lax.optimization_barrier((far, rows))

    def of_classes(value):
        value = lax.dynamic_slice_in_dim(value, h * half, half, 0)
        return jnp.where(c == 0, value, jnp.concatenate([value[quarter:], value[:quarter]]))[:, None]

    ids = (x * 2 + zl) * all_local + of_classes(jnp.arange(all_local, dtype=jnp.int32))
    labs = jnp.where(h == 0, jnp.concatenate([labels, labs]), jnp.concatenate([labs, labels]))[None, :]
    where = jnp.stack(places(ORDER[3:])).astype(jnp.int32)
    last_k, last_sq, ratio, slope, total = means_of(
        where, rows, far, swap(far, c=1), near_k, over_y, [swap(v, c=1) for v in over_y],
        of_classes(class_variance), of_classes(class_rate),
    )
    total = jnp.tile(total.reshape(1, 8, 128), (16, 1, 1))
    total = jnp.sum(lax.all_to_all(total, ("h", "x", "zl"), 0, 0, tiled=True), axis=0).reshape(1, -1)
    all_classes = all_local * 8
    intensity = (1.0 + total) / (1.0 + 0.5 * all_classes)

    def chunks(kept, came):
        parts = [slice(ky * 512, (ky + 1) * 512) for ky in range(4)]
        return [kept[:, at] + came[:, at].astype(F32) for at in parts]

    def over_y_rows(mine, came):
        near, back, far = (value.astype(F32) for value in came)
        return (mine + far) + (near + back)

    def slab_of(value, kz):
        kx = x ^ zh ^ kz
        return lax.dynamic_slice_in_dim(value, (kx ^ (kx // 2)) * SLAB, SLAB, 1)

    def outgoing(own):
        middle = lax.reduce_precision(jnp.mean(own, axis=1), 8, 7)
        rest = (own - middle[:, None]).astype(BF)
        tail = jnp.pad(middle.astype(BF), (0, 16 * SLAB - quarter)).reshape(16, SLAB)
        return [jnp.concatenate([slab_of(rest, kz), tail], 0) for kz in (2, 1, 3)]

    def incoming(value):
        middle = value[quarter:].reshape(-1)[:quarter]
        return value[:quarter].astype(F32) + middle.astype(F32)[:, None]

    def total_of(own, got):
        got = [incoming(value) for value in got]
        return jnp.stack([slab_of(own, 0) + got[0], got[1] + got[2]])

    kept, give = statistic(ratio, None, intensity, labs, ids, near_k, last_k)
    first = chunks(kept, swap(give, c=1))
    sent = [first[ky].astype(BF) for ky in (1, 3, 2)]
    came = [swap(value, y=ky) for value, ky in zip(sent, (1, 3, 2))]
    kept, give = statistic(ratio, slope, intensity, labs, ids, near_sq, last_sq)
    second = chunks(kept, swap(give, c=1))
    rest = [swap(second[ky].astype(BF), y=ky) for ky in (1, 3)]
    far, came[0] = lax.optimization_barrier((second[2].astype(BF), came[0]))
    rest.append(swap(far, y=2))

    first = over_y_rows(first[0], came)
    send = lax.optimization_barrier(outgoing(first))
    got = [swap(send[0], zh=2), swap(send[1], zh=1)]
    rest, got = lax.optimization_barrier((rest, got))
    late = send[2]
    second = over_y_rows(second[0], rest)
    send = lax.optimization_barrier(outgoing(second))
    both = swap(jnp.concatenate([send[2], late], 0), zh=3)
    first = total_of(first, got + [both[quarter + 16 :]])
    second = total_of(second, [swap(send[0], zh=2), swap(send[1], zh=1), both[: quarter + 16]])
    summed = jnp.stack([first, second]).transpose(0, 3, 1, 2) * (1.0 / (512 * 32))
    mine = lax.dynamic_slice_in_dim(summed, c * 64, 64, 1)
    theirs = swap(lax.dynamic_slice_in_dim(summed, (1 - c) * 64, 64, 1), c=1)

    def in_order(mine, theirs):
        pieces = []
        for half in range(2):
            same, other = (jnp.where(h == half, v[:, 0], v[:, 1]) for v in (mine, theirs))
            pieces += [jnp.where(c == 0, same, other), jnp.where(c == 0, other, same)]
        return jnp.concatenate(pieces, 1)

    return in_order(mine[0], theirs[0]), in_order(mine[1], theirs[1])


def solution(mesh):
    parts = Mesh(mesh.devices.reshape(tuple(SIZE.values())), AXES)
    dp, cls = ("g", "h", "y", "c"), ("x", "zl")
    in_specs = (P(dp, None), P(dp), P(cls, None), P(dp, cls), P(cls), P(cls))
    out_specs = (P(dp, cls), P(dp, cls))
    return jax.shard_map(body, mesh=parts, in_specs=in_specs, out_specs=out_specs, check_vma=False)
```

```python
import jax
import jax.numpy as jnp
from jax import lax
from jax.experimental import pallas as pl
from jax.experimental.pallas import tpu as pltpu
from jax.sharding import Mesh, PartitionSpec as P

SIZE = {"g": 2, "h": 2, "y": 4, "c": 2, "x": 4, "zl": 2}
AXES = tuple(SIZE)
BF = jnp.bfloat16
F32 = jnp.float32
SLAB = 128
ORDER = (0, 1, 3, 2)
PART = 128


def swap(value, zh=0, **masks):
    if zh:
        masks = dict(masks, g=zh // 2, h=zh % 2)
    masks = {a: m for a, m in masks.items() if m}
    names = tuple(a for a in AXES if a in masks)
    pairs, count = [], 1
    for a in names:
        count *= SIZE[a]
    for i in range(count):
        left, at = i, {}
        for a in reversed(names):
            at[a] = left % SIZE[a]
            left //= SIZE[a]
        j = 0
        for a in names:
            j = j * SIZE[a] + (at[a] ^ masks[a])
        pairs.append((i, j))
    return lax.ppermute(value, names, pairs)


def normalized(rows):
    values = rows.astype(F32)
    scale = lax.rsqrt(jnp.mean(values * values, axis=-1, keepdims=True) + 1e-06)
    return (values * scale).astype(BF)


def unit_slabs(at, points, features):
    def body(at, points, features, out, out_rows):
        out[...] = normalized(points[...])
        out_rows[...] = normalized(features[...])

    spec = lambda k: pl.BlockSpec((SLAB, points.shape[1]), lambda i, at: (at[k], 0))
    kept = pl.BlockSpec((SLAB, points.shape[1]), lambda i, at: (0, 0))
    shape = jax.ShapeDtypeStruct((SLAB, points.shape[1]), BF)
    grid = pltpu.PrefetchScalarGridSpec(
        num_scalar_prefetch=1, grid=(1,), in_specs=[spec(0), spec(1)], out_specs=[kept, kept]
    )
    return pl.pallas_call(body, grid_spec=grid, out_shape=[shape, shape], name="unit_slabs")(at, points, features)


def whole(value):
    return pl.BlockSpec(value.shape, lambda i: (0,) * value.ndim, pipeline_mode=pl.Buffered(1))


def stepped(body, name, steps, given, in_specs, out_shape, out_specs, scratch, flops):
    moved = 4 * sum(v.size for v in given)
    return pl.pallas_call(
        body,
        grid=(steps,),
        out_shape=out_shape,
        in_specs=in_specs,
        out_specs=out_specs,
        scratch_shapes=scratch,
        compiler_params=pltpu.CompilerParams(vmem_limit_bytes=48 << 20),
        cost_estimate=pl.CostEstimate(flops=flops, bytes_accessed=moved, transcendentals=0),
        name=name,
    )(*given)


def write_rows(left, table, place, first, factor, out, out_sq):
    dots = lax.dot_general(left, table, (((1,), (1,)), ((), ())), preferred_element_type=F32)
    value = jnp.exp(dots * factor).astype(BF)
    square = value * value
    for kl in range(2):
        to = pl.ds(pl.multiple_of(place[first + kl] * SLAB, SLAB), SLAB)
        out[:, to] = value[:, kl * SLAB : (kl + 1) * SLAB]
        out_sq[:, to] = square[:, kl * SLAB : (kl + 1) * SLAB]


def near_rows(places, features, relay, relay_far, pair, across, packs, across_packs):
    own, width = features.shape
    factor = 1.0 / float(width) ** 0.5
    step = 256

    def body(place, feature, relay, relay_far, pair, across, near, back, near_a, back_a, out, out_sq, rows_out, held):
        i = pl.program_id(0)

        @pl.when(i == 0)
        def _():
            held[pl.ds(pl.multiple_of(place[16] * own, own), own)] = normalized(feature[...])
            for k, rows in enumerate((relay, near, relay_far, back)):
                at = pl.ds(pl.multiple_of(place[12 + k] * PART, PART), PART)
                held[at] = rows[...] if k % 2 == 0 else rows[2 * SLAB :]

        left = held[pl.ds(pl.multiple_of(i * step, step), step)]
        rows_out[...] = left
        for n, table in enumerate((pair, across, near, near_a, back, back_a)):
            write_rows(left, table[: 2 * SLAB], place, 2 * n, factor, out, out_sq)

    given = [places, features, relay, relay_far, pair, across, *packs, *across_packs]
    shapes = [jax.ShapeDtypeStruct((2 * own, n), BF) for n in (12 * SLAB, 12 * SLAB, width)]
    return stepped(
        body,
        "near_rows",
        2 * own // step,
        given,
        [pl.BlockSpec(memory_space=pltpu.SMEM)] + [whole(v) for v in given[1:]],
        shapes,
        [pl.BlockSpec((step, s.shape[1]), lambda i: (i, 0)) for s in shapes],
        [pltpu.VMEM((2 * own, width), BF)],
        4 * own * 12 * SLAB * width,
    )


def means_of(places, rows, far, far_across, near_k, ours, theirs, variance, rate):
    count, width = rows.shape
    quarter = ours[0].shape[0]
    factor = 1.0 / float(width) ** 0.5
    step, cut = 512, 3 * SLAB

    def body(place, rows, far, far_across, near_k, *refs):
        blocks, (variance, rate, out, out_sq, ratio, slope, total, weights, held) = refs[:8], refs[8:]

        @pl.when(pl.program_id(0) == 0)
        def _():
            for k in range(2):
                here = slice(k * quarter, (k + 1) * quarter)
                for ky in range(4):
                    block = blocks[4 * k + ky]
                    weights[here, ky * cut : (ky + 1) * cut] = block[:, :cut]
                    weights[here, 12 * SLAB + ky * SLAB : 12 * SLAB + (ky + 1) * SLAB] = block[:, cut:]

        for n, table in enumerate((far, far_across)):
            write_rows(rows[...], table[...], place, 2 * n, factor, out, out_sq)
        transposed = (((1,), (1,)), ((), ()))
        held[...] = lax.dot_general(
            weights[:, : 12 * SLAB], near_k[...], transposed, preferred_element_type=F32
        ) + lax.dot_general(weights[:, 12 * SLAB :], out[...], transposed, preferred_element_type=F32)
        part = jnp.zeros((1, step), F32)
        for k in range(4):
            here = slice(k * quarter // 2, (k + 1) * quarter // 2)
            means = held[here]
            square = means * means + variance[here]
            inverse = lax.rsqrt(square)
            spread = square * inverse
            small = jnp.exp(-spread)
            share = 1.0 / (1.0 + small)
            value = rate[here] * jnp.exp(-(means + spread) * 0.5) * share
            ratio[here] = value
            slope[here] = (1.0 - small) * share * (0.5 * inverse)
            part += jnp.sum(value, axis=0, keepdims=True)
        total[...] = part

    given = [places, rows, far, far_across, near_k, *ours, *theirs, variance, rate]
    wide = jax.ShapeDtypeStruct((2 * quarter, count), F32)
    last = jax.ShapeDtypeStruct((count, 4 * SLAB), BF)
    by_rows = lambda v: pl.BlockSpec((step, v.shape[1]), lambda i: (i, 0))
    by_columns = lambda v: pl.BlockSpec((v.shape[0], step), lambda i: (0, i))
    total = jax.ShapeDtypeStruct((1, count), F32)
    return stepped(
        body,
        "means",
        count // step,
        given,
        [pl.BlockSpec(memory_space=pltpu.SMEM), by_rows(rows), whole(far), whole(far_across), by_rows(near_k)]
        + [whole(v) for v in given[5:]],
        [pltpu.HBM(last.shape, BF), pltpu.HBM(last.shape, BF), wide, wide, total],
        [by_rows(last), by_rows(last), by_columns(wide), by_columns(wide), by_columns(total)],
        [pltpu.VMEM((2 * quarter, 16 * SLAB), BF), pltpu.VMEM((2 * quarter, step), F32)],
        2 * count * 16 * SLAB * 2 * quarter,
    )


def statistic(ratio, slope, intensity, labels, ids, near, last):
    quarter, count = ratio.shape[0] // 2, ratio.shape[1]
    steps = 2

    def body(*refs):
        ratio, slope = refs[0], refs[1] if slopes else None
        intensity, labels, ids, near, last, keep, give, weight, joint = refs[1 + len(slopes) :]

        @pl.when(pl.program_id(0) == 0)
        def _():
            for k in range(4):
                here = slice(k * quarter // 2, (k + 1) * quarter // 2)
                hot = (ids[here] == labels[...]).astype(F32)
                expected = intensity[...] * ratio[here]
                value = (hot - expected) * 0.5 if slope is None else (hot + expected) * slope[here]
                weight[here] = value.astype(BF)

        for k in range(2):
            joint[:, 4 * k * SLAB : (4 * k + 3) * SLAB] = near[:, 3 * k * SLAB : 3 * (k + 1) * SLAB]
            joint[:, (4 * k + 3) * SLAB : 4 * (k + 1) * SLAB] = last[:, k * SLAB : (k + 1) * SLAB]
        sums = jnp.dot(weight[...], joint[...], preferred_element_type=F32)
        keep[...] = sums[:quarter]
        give[...] = sums[quarter:].astype(BF)

    slopes = [] if slope is None else [slope]
    last = pltpu.with_memory_space_constraint(last, pltpu.HBM)
    given = [ratio, *slopes, intensity, labels, ids, near, last]
    block = lambda rows, cols: pl.BlockSpec((rows, cols), lambda i: (0, i))
    return stepped(
        body,
        "statistic",
        steps,
        given,
        [whole(v) for v in given[:-2]] + [block(count, 6 * SLAB), block(count, 2 * SLAB)],
        [jax.ShapeDtypeStruct((quarter, 16 * SLAB), F32), jax.ShapeDtypeStruct((quarter, 16 * SLAB), BF)],
        [block(quarter, 8 * SLAB), block(quarter, 8 * SLAB)],
        [pltpu.VMEM(ratio.shape, BF), pltpu.VMEM((count, 8 * SLAB), BF)],
        2 * count * 16 * SLAB * 2 * quarter,
    )


def body(features, labels, inducing, mean_weights, class_variance, class_rate):
    g, h, y, c, x, zl = (lax.axis_index(a) for a in AXES)
    zh = 2 * g + h
    all_local = mean_weights.shape[1]
    half = all_local // 2
    quarter = half // 2

    mine, relay = unit_slabs(jnp.stack([c, x]).astype(jnp.int32), inducing, features)
    mine, relay, mean_weights = lax.optimization_barrier((mine, relay, mean_weights))
    relay = swap(relay, zh=1)
    labs = swap(labels, zh=1)
    pair = jnp.concatenate([mine, swap(mine, zl=1)], 0)

    local = mean_weights.T.reshape(2, 2, quarter, -1)
    keep = lax.dynamic_index_in_dim(local, c, 1, False)
    give = lax.dynamic_index_in_dim(local, 1 - c, 1, False)
    got = swap(give, c=1)
    block = jnp.where(c == 0, jnp.concatenate([keep, got], 2), jnp.concatenate([got, keep], 2))
    same = lax.dynamic_index_in_dim(block, h, 0, False)
    other = lax.dynamic_index_in_dim(block, 1 - h, 0, False)
    over_z = jnp.stack([same, swap(other, zh=1), swap(same, zh=2), swap(other, zh=3)])
    over_z = jnp.concatenate([lax.dynamic_index_in_dim(over_z, zh ^ x ^ kx, 0, False) for kx in ORDER], 1)

    pack = jnp.concatenate([pair, relay], 0)
    near, back = swap(pack, x=1), swap(pack, x=3)
    over_z, pack = lax.optimization_barrier((over_z, pack))
    over_y = [over_z, swap(over_z, y=1), None, swap(over_z, y=3)]
    relay_far, near, back, pair, labs, over_z, over_y[1], over_y[3] = lax.optimization_barrier(
        (swap(relay, x=2), near, back, pair, labs, over_z, over_y[1], over_y[3])
    )
    over_y[2] = swap(over_z, y=2)
    far = swap(pair, x=2)

    def places(order):
        found = []
        for i, kx in enumerate(order):
            for core in (c, 1 - c):
                for kl in range(2):
                    found.append((y ^ ((zl ^ kl) * 2 + core)) * len(order) + i)
        return found

    where = places(ORDER[:3]) + [(1 - h) * 4 + (x ^ kx) for kx in range(4)] + [h]
    where = jnp.stack(where).astype(jnp.int32)
    across = (swap(near, c=1), swap(back, c=1))
    near_k, near_sq, rows = near_rows(where, features, relay, relay_far, pair, swap(pair, c=1), (near, back), across)
    far, rows = lax.optimization_barrier((far, rows))

    def of_classes(value):
        value = lax.dynamic_slice_in_dim(value, h * half, half, 0)
        return jnp.where(c == 0, value, jnp.concatenate([value[quarter:], value[:quarter]]))[:, None]

    ids = (x * 2 + zl) * all_local + of_classes(jnp.arange(all_local, dtype=jnp.int32))
    labs = jnp.where(h == 0, jnp.concatenate([labels, labs]), jnp.concatenate([labs, labels]))[None, :]
    where = jnp.stack(places(ORDER[3:])).astype(jnp.int32)
    last_k, last_sq, ratio, slope, total = means_of(
        where, rows, far, swap(far, c=1), near_k, over_y, [swap(v, c=1) for v in over_y],
        of_classes(class_variance), of_classes(class_rate),
    )
    total = jnp.tile(total.reshape(1, 8, 128), (16, 1, 1))
    total = jnp.sum(lax.all_to_all(total, ("h", "x", "zl"), 0, 0, tiled=True), axis=0).reshape(1, -1)
    all_classes = all_local * 8
    intensity = (1.0 + total) / (1.0 + 0.5 * all_classes)

    def chunks(kept, came):
        parts = [slice(ky * 512, (ky + 1) * 512) for ky in range(4)]
        return [kept[:, at] + came[:, at].astype(F32) for at in parts]

    def over_y_rows(mine, came):
        near, back, far = (value.astype(F32) for value in came)
        return (mine + far) + (near + back)

    def slab_of(value, kz):
        kx = x ^ zh ^ kz
        return lax.dynamic_slice_in_dim(value, (kx ^ (kx // 2)) * SLAB, SLAB, 1)

    def outgoing(own):
        middle = lax.reduce_precision(jnp.mean(own, axis=1), 8, 7)
        rest = (own - middle[:, None]).astype(BF)
        tail = jnp.pad(middle.astype(BF), (0, 16 * SLAB - quarter)).reshape(16, SLAB)
        return [jnp.concatenate([slab_of(rest, kz), tail], 0) for kz in (2, 1, 3)]

    def incoming(value):
        middle = value[quarter:].reshape(-1)[:quarter]
        return value[:quarter].astype(F32) + middle.astype(F32)[:, None]

    def total_of(own, got):
        got = [incoming(value) for value in got]
        return jnp.stack([slab_of(own, 0) + got[0], got[1] + got[2]])

    kept, give = statistic(ratio, None, intensity, labs, ids, near_k, last_k)
    first = chunks(kept, swap(give, c=1))
    sent = [first[ky].astype(BF) for ky in (1, 3, 2)]
    came = [swap(value, y=ky) for value, ky in zip(sent, (1, 3, 2))]
    kept, give = statistic(ratio, slope, intensity, labs, ids, near_sq, last_sq)
    second = chunks(kept, swap(give, c=1))
    rest = [swap(second[ky].astype(BF), y=ky) for ky in (1, 3)]
    far, came[0] = lax.optimization_barrier((second[2].astype(BF), came[0]))
    rest.append(swap(far, y=2))

    first = over_y_rows(first[0], came)
    send = lax.optimization_barrier(outgoing(first))
    got = [swap(send[0], zh=2), swap(send[1], zh=1)]
    rest, got = lax.optimization_barrier((rest, got))
    late = send[2]
    second = over_y_rows(second[0], rest)
    send = lax.optimization_barrier(outgoing(second))
    both = swap(jnp.concatenate([send[2], late], 0), zh=3)
    first = total_of(first, got + [both[quarter + 16 :]])
    second = total_of(second, [swap(send[0], zh=2), swap(send[1], zh=1), both[: quarter + 16]])
    summed = jnp.stack([first, second]).transpose(0, 3, 1, 2) * (1.0 / (512 * 32))
    mine = lax.dynamic_slice_in_dim(summed, c * 64, 64, 1)
    theirs = swap(lax.dynamic_slice_in_dim(summed, (1 - c) * 64, 64, 1), c=1)

    def in_order(mine, theirs):
        pieces = []
        for half in range(2):
            same, other = (jnp.where(h == half, v[:, 0], v[:, 1]) for v in (mine, theirs))
            pieces += [jnp.where(c == 0, same, other), jnp.where(c == 0, other, same)]
        return jnp.concatenate(pieces, 1)

    return in_order(mine[0], theirs[0]), in_order(mine[1], theirs[1])


def solution(mesh):
    parts = Mesh(mesh.devices.reshape(tuple(SIZE.values())), AXES)
    dp, cls = ("g", "h", "y", "c"), ("x", "zl")
    in_specs = (P(dp, None), P(dp), P(cls, None), P(dp, cls), P(cls), P(cls))
    out_specs = (P(dp, cls), P(dp, cls))
    return jax.shard_map(body, mesh=parts, in_specs=in_specs, out_specs=out_specs, check_vma=False)
```

```python
import jax
import jax.numpy as jnp
from jax import lax
from jax.experimental import pallas as pl
from jax.experimental.pallas import tpu as pltpu
from jax.sharding import Mesh, PartitionSpec as P

SIZE = {"g": 2, "h": 2, "y": 4, "c": 2, "x": 4, "zl": 2}
AXES = tuple(SIZE)
BF = jnp.bfloat16
F32 = jnp.float32
SLAB = 128
ORDER = (0, 1, 3, 2)
PART = 128


def swap(value, zh=0, **masks):
    if zh:
        masks = dict(masks, g=zh // 2, h=zh % 2)
    masks = {a: m for a, m in masks.items() if m}
    names = tuple(a for a in AXES if a in masks)
    pairs, count = [], 1
    for a in names:
        count *= SIZE[a]
    for i in range(count):
        left, at = i, {}
        for a in reversed(names):
            at[a] = left % SIZE[a]
            left //= SIZE[a]
        j = 0
        for a in names:
            j = j * SIZE[a] + (at[a] ^ masks[a])
        pairs.append((i, j))
    return lax.ppermute(value, names, pairs)


def normalized(rows):
    values = rows.astype(F32)
    scale = lax.rsqrt(jnp.mean(values * values, axis=-1, keepdims=True) + 1e-06)
    return (values * scale).astype(BF)


def unit_slabs(at, points, features):
    def body(at, points, features, out, out_rows):
        out[...] = normalized(points[...])
        out_rows[...] = normalized(features[...])

    spec = lambda k: pl.BlockSpec((SLAB, points.shape[1]), lambda i, at: (at[k], 0))
    kept = pl.BlockSpec((SLAB, points.shape[1]), lambda i, at: (0, 0))
    shape = jax.ShapeDtypeStruct((SLAB, points.shape[1]), BF)
    grid = pltpu.PrefetchScalarGridSpec(
        num_scalar_prefetch=1, grid=(1,), in_specs=[spec(0), spec(1)], out_specs=[kept, kept]
    )
    return pl.pallas_call(body, grid_spec=grid, out_shape=[shape, shape], name="unit_slabs")(at, points, features)


def whole(value):
    return pl.BlockSpec(value.shape, lambda i: (0,) * value.ndim, pipeline_mode=pl.Buffered(1))


def stepped(body, name, steps, given, in_specs, out_shape, out_specs, scratch, flops):
    moved = 4 * sum(v.size for v in given)
    return pl.pallas_call(
        body,
        grid=(steps,),
        out_shape=out_shape,
        in_specs=in_specs,
        out_specs=out_specs,
        scratch_shapes=scratch,
        compiler_params=pltpu.CompilerParams(vmem_limit_bytes=48 << 20),
        cost_estimate=pl.CostEstimate(flops=flops, bytes_accessed=moved, transcendentals=0),
        name=name,
    )(*given)


def write_rows(left, table, place, first, factor, out, out_sq):
    dots = lax.dot_general(left, table, (((1,), (1,)), ((), ())), preferred_element_type=F32)
    value = jnp.exp(dots * factor).astype(BF)
    square = value * value
    for kl in range(2):
        to = pl.ds(pl.multiple_of(place[first + kl] * SLAB, SLAB), SLAB)
        out[:, to] = value[:, kl * SLAB : (kl + 1) * SLAB]
        out_sq[:, to] = square[:, kl * SLAB : (kl + 1) * SLAB]


def near_rows(places, features, relay, relay_far, pair, across, packs, across_packs):
    own, width = features.shape
    factor = 1.0 / float(width) ** 0.5
    step = 256

    def body(place, feature, relay, relay_far, pair, across, near, back, near_a, back_a, out, out_sq, rows_out, held):
        i = pl.program_id(0)

        @pl.when(i == 0)
        def _():
            held[pl.ds(pl.multiple_of(place[16] * own, own), own)] = normalized(feature[...])
            for k, rows in enumerate((relay, near, relay_far, back)):
                at = pl.ds(pl.multiple_of(place[12 + k] * PART, PART), PART)
                held[at] = rows[...] if k % 2 == 0 else rows[2 * SLAB :]

        left = held[pl.ds(pl.multiple_of(i * step, step), step)]
        rows_out[...] = left
        for n, table in enumerate((pair, across, near, near_a, back, back_a)):
            write_rows(left, table[: 2 * SLAB], place, 2 * n, factor, out, out_sq)

    given = [places, features, relay, relay_far, pair, across, *packs, *across_packs]
    shapes = [jax.ShapeDtypeStruct((2 * own, n), BF) for n in (12 * SLAB, 12 * SLAB, width)]
    return stepped(
        body,
        "near_rows",
        2 * own // step,
        given,
        [pl.BlockSpec(memory_space=pltpu.SMEM)] + [whole(v) for v in given[1:]],
        shapes,
        [pl.BlockSpec((step, s.shape[1]), lambda i: (i, 0)) for s in shapes],
        [pltpu.VMEM((2 * own, width), BF)],
        4 * own * 12 * SLAB * width,
    )


def means_of(places, rows, far, far_across, near_k, ours, theirs, variance, rate):
    count, width = rows.shape
    quarter = ours[0].shape[0]
    factor = 1.0 / float(width) ** 0.5
    step, cut = 256, 3 * SLAB

    def body(place, rows, far, far_across, near_k, *refs):
        blocks, (variance, rate, out, out_sq, ratio, slope, total, weights, held) = refs[:8], refs[8:]

        @pl.when(pl.program_id(0) == 0)
        def _():
            for k in range(2):
                here = slice(k * quarter, (k + 1) * quarter)
                for ky in range(4):
                    block = blocks[4 * k + ky]
                    weights[here, ky * cut : (ky + 1) * cut] = block[:, :cut]
                    weights[here, 12 * SLAB + ky * SLAB : 12 * SLAB + (ky + 1) * SLAB] = block[:, cut:]

        for n, table in enumerate((far, far_across)):
            write_rows(rows[...], table[...], place, 2 * n, factor, out, out_sq)
        transposed = (((1,), (1,)), ((), ()))
        held[...] = lax.dot_general(
            weights[:, : 12 * SLAB], near_k[...], transposed, preferred_element_type=F32
        ) + lax.dot_general(weights[:, 12 * SLAB :], out[...], transposed, preferred_element_type=F32)
        part = jnp.zeros((1, step), F32)
        for k in range(4):
            here = slice(k * quarter // 2, (k + 1) * quarter // 2)
            means = held[here]
            square = means * means + variance[here]
            inverse = lax.rsqrt(square)
            spread = square * inverse
            small = jnp.exp(-spread)
            share = 1.0 / (1.0 + small)
            value = rate[here] * jnp.exp(-(means + spread) * 0.5) * share
            ratio[here] = value
            slope[here] = (1.0 - small) * share * (0.5 * inverse)
            part += jnp.sum(value, axis=0, keepdims=True)
        total[...] = part

    given = [places, rows, far, far_across, near_k, *ours, *theirs, variance, rate]
    wide = jax.ShapeDtypeStruct((2 * quarter, count), F32)
    last = jax.ShapeDtypeStruct((count, 4 * SLAB), BF)
    by_rows = lambda v: pl.BlockSpec((step, v.shape[1]), lambda i: (i, 0))
    by_columns = lambda v: pl.BlockSpec((v.shape[0], step), lambda i: (0, i))
    total = jax.ShapeDtypeStruct((1, count), F32)
    return stepped(
        body,
        "means",
        count // step,
        given,
        [pl.BlockSpec(memory_space=pltpu.SMEM), by_rows(rows), whole(far), whole(far_across), by_rows(near_k)]
        + [whole(v) for v in given[5:]],
        [pltpu.HBM(last.shape, BF), pltpu.HBM(last.shape, BF), wide, wide, total],
        [by_rows(last), by_rows(last), by_columns(wide), by_columns(wide), by_columns(total)],
        [pltpu.VMEM((2 * quarter, 16 * SLAB), BF), pltpu.VMEM((2 * quarter, step), F32)],
        2 * count * 16 * SLAB * 2 * quarter,
    )


def statistic(ratio, slope, intensity, labels, ids, near, last):
    quarter, count = ratio.shape[0] // 2, ratio.shape[1]
    steps = 2

    def body(*refs):
        ratio, slope = refs[0], refs[1] if slopes else None
        intensity, labels, ids, near, last, keep, give, weight, joint = refs[1 + len(slopes) :]

        @pl.when(pl.program_id(0) == 0)
        def _():
            for k in range(4):
                here = slice(k * quarter // 2, (k + 1) * quarter // 2)
                hot = (ids[here] == labels[...]).astype(F32)
                expected = intensity[...] * ratio[here]
                value = (hot - expected) * 0.5 if slope is None else (hot + expected) * slope[here]
                weight[here] = value.astype(BF)

        for k in range(2):
            joint[:, 4 * k * SLAB : (4 * k + 3) * SLAB] = near[:, 3 * k * SLAB : 3 * (k + 1) * SLAB]
            joint[:, (4 * k + 3) * SLAB : 4 * (k + 1) * SLAB] = last[:, k * SLAB : (k + 1) * SLAB]
        sums = jnp.dot(weight[...], joint[...], preferred_element_type=F32)
        keep[...] = sums[:quarter]
        give[...] = sums[quarter:].astype(BF)

    slopes = [] if slope is None else [slope]
    last = pltpu.with_memory_space_constraint(last, pltpu.HBM)
    given = [ratio, *slopes, intensity, labels, ids, near, last]
    block = lambda rows, cols: pl.BlockSpec((rows, cols), lambda i: (0, i))
    return stepped(
        body,
        "statistic",
        steps,
        given,
        [whole(v) for v in given[:-2]] + [block(count, 6 * SLAB), block(count, 2 * SLAB)],
        [jax.ShapeDtypeStruct((quarter, 16 * SLAB), F32), jax.ShapeDtypeStruct((quarter, 16 * SLAB), BF)],
        [block(quarter, 8 * SLAB), block(quarter, 8 * SLAB)],
        [pltpu.VMEM(ratio.shape, BF), pltpu.VMEM((count, 8 * SLAB), BF)],
        2 * count * 16 * SLAB * 2 * quarter,
    )


def body(features, labels, inducing, mean_weights, class_variance, class_rate):
    g, h, y, c, x, zl = (lax.axis_index(a) for a in AXES)
    zh = 2 * g + h
    all_local = mean_weights.shape[1]
    half = all_local // 2
    quarter = half // 2

    mine, relay = unit_slabs(jnp.stack([c, x]).astype(jnp.int32), inducing, features)
    mine, relay, mean_weights = lax.optimization_barrier((mine, relay, mean_weights))
    relay = swap(relay, zh=1)
    labs = swap(labels, zh=1)
    pair = jnp.concatenate([mine, swap(mine, zl=1)], 0)

    local = mean_weights.T.reshape(2, 2, quarter, -1)
    keep = lax.dynamic_index_in_dim(local, c, 1, False)
    give = lax.dynamic_index_in_dim(local, 1 - c, 1, False)
    got = swap(give, c=1)
    block = jnp.where(c == 0, jnp.concatenate([keep, got], 2), jnp.concatenate([got, keep], 2))
    same = lax.dynamic_index_in_dim(block, h, 0, False)
    other = lax.dynamic_index_in_dim(block, 1 - h, 0, False)
    over_z = jnp.stack([same, swap(other, zh=1), swap(same, zh=2), swap(other, zh=3)])
    over_z = jnp.concatenate([lax.dynamic_index_in_dim(over_z, zh ^ x ^ kx, 0, False) for kx in ORDER], 1)

    pack = jnp.concatenate([pair, relay], 0)
    near, back = swap(pack, x=1), swap(pack, x=3)
    over_z, pack = lax.optimization_barrier((over_z, pack))
    over_y = [over_z, swap(over_z, y=1), None, swap(over_z, y=3)]
    relay_far, near, back, pair, labs, over_z, over_y[1], over_y[3] = lax.optimization_barrier(
        (swap(relay, x=2), near, back, pair, labs, over_z, over_y[1], over_y[3])
    )
    over_y[2] = swap(over_z, y=2)
    far = swap(pair, x=2)

    def places(order):
        found = []
        for i, kx in enumerate(order):
            for core in (c, 1 - c):
                for kl in range(2):
                    found.append((y ^ ((zl ^ kl) * 2 + core)) * len(order) + i)
        return found

    where = places(ORDER[:3]) + [(1 - h) * 4 + (x ^ kx) for kx in range(4)] + [h]
    where = jnp.stack(where).astype(jnp.int32)
    across = (swap(near, c=1), swap(back, c=1))
    near_k, near_sq, rows = near_rows(where, features, relay, relay_far, pair, swap(pair, c=1), (near, back), across)
    far, rows = lax.optimization_barrier((far, rows))

    def of_classes(value):
        value = lax.dynamic_slice_in_dim(value, h * half, half, 0)
        return jnp.where(c == 0, value, jnp.concatenate([value[quarter:], value[:quarter]]))[:, None]

    ids = (x * 2 + zl) * all_local + of_classes(jnp.arange(all_local, dtype=jnp.int32))
    labs = jnp.where(h == 0, jnp.concatenate([labels, labs]), jnp.concatenate([labs, labels]))[None, :]
    where = jnp.stack(places(ORDER[3:])).astype(jnp.int32)
    last_k, last_sq, ratio, slope, total = means_of(
        where, rows, far, swap(far, c=1), near_k, over_y, [swap(v, c=1) for v in over_y],
        of_classes(class_variance), of_classes(class_rate),
    )
    total = jnp.tile(total.reshape(1, 8, 128), (16, 1, 1))
    total = jnp.sum(lax.all_to_all(total, ("h", "x", "zl"), 0, 0, tiled=True), axis=0).reshape(1, -1)
    all_classes = all_local * 8
    intensity = (1.0 + total) / (1.0 + 0.5 * all_classes)

    def chunks(kept, came):
        parts = [slice(ky * 512, (ky + 1) * 512) for ky in range(4)]
        return [kept[:, at] + came[:, at].astype(F32) for at in parts]

    def over_y_rows(mine, came):
        near, back, far = (value.astype(F32) for value in came)
        return (mine + far) + (near + back)

    def slab_of(value, kz):
        kx = x ^ zh ^ kz
        return lax.dynamic_slice_in_dim(value, (kx ^ (kx // 2)) * SLAB, SLAB, 1)

    def outgoing(own):
        middle = lax.reduce_precision(jnp.mean(own, axis=1), 8, 7)
        rest = (own - middle[:, None]).astype(BF)
        tail = jnp.pad(middle.astype(BF), (0, 16 * SLAB - quarter)).reshape(16, SLAB)
        return [jnp.concatenate([slab_of(rest, kz), tail], 0) for kz in (2, 1, 3)]

    def incoming(value):
        middle = value[quarter:].reshape(-1)[:quarter]
        return value[:quarter].astype(F32) + middle.astype(F32)[:, None]

    def total_of(own, got):
        got = [incoming(value) for value in got]
        return jnp.stack([slab_of(own, 0) + got[0], got[1] + got[2]])

    kept, give = statistic(ratio, None, intensity, labs, ids, near_k, last_k)
    first = chunks(kept, swap(give, c=1))
    sent = [first[ky].astype(BF) for ky in (1, 3, 2)]
    came = [swap(value, y=ky) for value, ky in zip(sent, (1, 3, 2))]
    kept, give = statistic(ratio, slope, intensity, labs, ids, near_sq, last_sq)
    second = chunks(kept, swap(give, c=1))
    rest = [swap(second[ky].astype(BF), y=ky) for ky in (1, 3)]
    far, came[0] = lax.optimization_barrier((second[2].astype(BF), came[0]))
    rest.append(swap(far, y=2))

    first = over_y_rows(first[0], came)
    send = lax.optimization_barrier(outgoing(first))
    got = [swap(send[0], zh=2), swap(send[1], zh=1)]
    rest, got = lax.optimization_barrier((rest, got))
    late = send[2]
    second = over_y_rows(second[0], rest)
    send = lax.optimization_barrier(outgoing(second))
    both = swap(jnp.concatenate([send[2], late], 0), zh=3)
    first = total_of(first, got + [both[quarter + 16 :]])
    second = total_of(second, [swap(send[0], zh=2), swap(send[1], zh=1), both[: quarter + 16]])
    summed = jnp.stack([first, second]).transpose(0, 3, 1, 2) * (1.0 / (512 * 32))
    mine = lax.dynamic_slice_in_dim(summed, c * 64, 64, 1)
    theirs = swap(lax.dynamic_slice_in_dim(summed, (1 - c) * 64, 64, 1), c=1)

    def in_order(mine, theirs):
        pieces = []
        for half in range(2):
            same, other = (jnp.where(h == half, v[:, 0], v[:, 1]) for v in (mine, theirs))
            pieces += [jnp.where(c == 0, same, other), jnp.where(c == 0, other, same)]
        return jnp.concatenate(pieces, 1)

    return in_order(mine[0], theirs[0]), in_order(mine[1], theirs[1])


def solution(mesh):
    parts = Mesh(mesh.devices.reshape(tuple(SIZE.values())), AXES)
    dp, cls = ("g", "h", "y", "c"), ("x", "zl")
    in_specs = (P(dp, None), P(dp), P(cls, None), P(dp, cls), P(cls), P(cls))
    out_specs = (P(dp, cls), P(dp, cls))
    return jax.shard_map(body, mesh=parts, in_specs=in_specs, out_specs=out_specs, check_vma=False)
```
